128 devices in a mesh: gx: 16 (over y_lo, x, core), gz: 8 (over z, y_hi).
Axes of the slice: x: 4, y: 4 (y_hi: 2, y_lo: 2; y = y_hi * 2 + y_lo), z: 4, core: 2. Of those that a mesh axis runs over, the one named last changes fastest.
Arguments:
- face_residual: float32 [2, 6, 121, 16, 2048], P(None, None, None, 'gx', 'gz'), may hold values from -6 to 6
- edge_residual: float32 [2, 12, 11, 16, 2048], P(None, None, None, 'gx', 'gz'), may hold values from -6 to 6
- vertex_residual: float32 [2, 8, 16, 2048], P(None, None, 'gx', 'gz'), may hold values from -6 to 6
- face_orient: int32 [6, 16, 2048], P(None, 'gx', 'gz'), may hold values from 0 to 7
- edge_orient: int32 [12, 16, 2048], P(None, 'gx', 'gz'), may hold values from 0 to 1
- stiffness: float32 [16, 2048], P('gx', 'gz'), may hold values from 0.3 to 3
- face_basis: float32 [11, 11], replicated, may hold values from -0.3 to 1.3
- face_eigs: float32 [11], replicated, may hold values from 0.3 to 60
- extension: float32 [121, 48], replicated, may hold values from -0.875 to 0.875
- edge_diag: float32 [11], replicated, may hold values from 1 to 4
- element_heights: float32 [32], replicated, may hold values from 0.2 to 2
Outputs:
- face_solution: float32 [2, 6, 121, 16, 2048], P(None, None, None, 'gx', 'gz')
- edge_solution: float32 [2, 12, 11, 16, 2048], P(None, None, None, 'gx', 'gz')
- vertex_solution: float32 [2, 8, 16, 2048], P(None, None, 'gx', 'gz')
The draws below stay inside these ranges and needn't reach their ends.
All inputs are finite; a program needn't handle non-finite values.
Results may differ from the reference program's by a relative error of at most 0.0003.
Values sent between devices are 32-bit elements; how exact they have to be, the bound alone decides.
No kernel may reach another device: no remote copies, remote signals or barrier semaphores. Data moves between devices by JAX's collectives and lax.ppermute only.
A program may use at most 192 MiB of HBM per device.

```python
import math
import jax
import jax.numpy as jnp
from jax import lax

SOLVES = 2
NODES = 11
LAYERS = 32
FACE_NODES = 121
BOUNDARY = 48
SPAN_X = 16
SPAN_Z = 64
COLUMNS = 2048


def draw_face_basis(key, part):
    key = jax.random.fold_in(key, 11)
    spread = 0.09 * jnp.clip(jax.random.normal(key, (NODES, NODES), jnp.float32), -3.0, 3.0)
    return jnp.eye(NODES, dtype=jnp.float32) + spread


def plant(values, key, least, high):
    dims = values.shape
    index_at = [jax.random.randint(jax.random.fold_in(key, axis), (), 0, dims[axis]) for axis in range(len(dims))]
    values = values.at[tuple(index_at)].set(least)
    longest = dims.index(max(dims))
    index_at[longest] = (index_at[longest] + 1) % dims[longest]
    return values.at[tuple(index_at)].set(high)


def levels(stream_key, shape, split, low, largest):
    level, own = 1.0, jax.random.fold_in(stream_key, 6)
    for dim, parts in split:
        draws = jnp.exp(jax.random.uniform(jax.random.fold_in(own, dim), (parts,), jnp.float32, low / len(split), largest / len(split)))
        level = level * jnp.repeat(draws, shape[dim] // parts).reshape([-1 if axis == dim else 1 for axis in range(len(shape))])
    return level


def normal_values(key, shape, deviation, reach, cuts=(), kind=jnp.bfloat16):
    values = deviation * jax.random.normal(key, shape, jnp.float32)
    if cuts:
        values = values * levels(key, shape, cuts, -0.22, 0.18)
    return jnp.clip(values, -reach, reach).astype(kind)


def setup_inputs(seed: int = 0) -> dict:
    seeds = jax.random.split(jax.random.key(seed), 12)
    return {
        "face_residual": normal_values(seeds[0], (SOLVES, 6, FACE_NODES, SPAN_X, COLUMNS), 1.0, 6.0, ((3, 16), (4, 8)), jnp.float32),
        "edge_residual": normal_values(seeds[1], (SOLVES, 12, NODES, SPAN_X, COLUMNS), 1.0, 6.0, ((3, 16), (4, 8)), jnp.float32),
        "vertex_residual": normal_values(seeds[2], (SOLVES, 8, SPAN_X, COLUMNS), 1.0, 6.0, ((2, 16), (3, 8)), jnp.float32),
        "face_orient": plant(jax.random.randint(seeds[3], (6, SPAN_X, COLUMNS), 0, 8), jax.random.fold_in(seeds[3], 1), 0, 7).astype(jnp.int32),
        "edge_orient": plant(jax.random.randint(seeds[4], (12, SPAN_X, COLUMNS), 0, 2), jax.random.fold_in(seeds[4], 1), 0, 1).astype(jnp.int32),
        "stiffness": jnp.clip(jnp.exp(math.log(3.0) - 2.3025851 * jax.random.uniform(seeds[5], (SPAN_X, COLUMNS), jnp.float32) ** levels(seeds[5], (SPAN_X, COLUMNS), ((0, 16), (1, 8)), -0.2, 0.2)), 0.3, 3.0),
        "face_basis": draw_face_basis(jax.random.fold_in(seeds[11], 71), 0),
        "face_eigs": jnp.clip(jnp.exp(jax.random.uniform(seeds[7], (NODES,), jnp.float32, math.log(0.3), math.log(60.0))), 0.3, 60.0),
        "extension": normal_values(seeds[8], (FACE_NODES, BOUNDARY), BOUNDARY ** -0.5, 0.875, (), jnp.float32),
        "edge_diag": jnp.clip(jnp.exp(jax.random.uniform(seeds[9], (NODES,), jnp.float32, math.log(1.0), math.log(4.0))), 1.0, 4.0),
        "element_heights": jnp.clip(jnp.exp(jax.random.uniform(seeds[10], (LAYERS,), jnp.float32, math.log(0.2), math.log(2.0))), 0.2, 2.0),
    }


FACE_SLOTS = ((-1, 0, 0), (1, 0, 0), (0, -1, 0), (0, 1, 0), (0, 0, -1), (0, 0, 1))
EDGE_SLOTS = ((0, -1, -1), (0, -1, 1), (0, 1, -1), (0, 1, 1), (-1, 0, -1), (-1, 0, 1), (1, 0, -1), (1, 0, 1), (-1, -1, 0), (-1, 1, 0), (1, -1, 0), (1, 1, 0))
VERTEX_SLOTS = ((-1, -1, -1), (-1, -1, 1), (-1, 1, -1), (-1, 1, 1), (1, -1, -1), (1, -1, 1), (1, 1, -1), (1, 1, 1))
shift_mass = 0.004
HIGHEST = lax.Precision.HIGHEST

def moves_of(slot):
    result = [()]
    for part in slot:
        options = (0,) if part == 0 else (0, part)
        result = [prior + (option,) for prior in result for option in options]
    return result

def partner_of(slot, move):
    return tuple((part - 2 * step for part, step in zip(slot, move)))

def shift_levels(array, step):
    if step == 0:
        return array
    zeros = jnp.zeros(array.shape[:-1] + (1,), array.dtype)
    if step > 0:
        return jnp.concatenate([array[..., 1:], zeros], axis=-1)
    return jnp.concatenate([zeros, array[..., :-1]], axis=-1)

def sum_slots(slots, fetch):
    totals = []
    for slot in slots:
        total = None
        for move in moves_of(slot):
            term = fetch(slots.index(partner_of(slot, move)), move)
            total = term if total is None else total + term
        totals.append(total)
    return totals

def faces_to_frame(values, turn):
    turn = turn[None, :, None, None]
    values = jnp.where(turn // 4 % 2 == 1, jnp.swapaxes(values, 2, 3), values)
    values = jnp.where(turn % 2 == 1, jnp.flip(values, 2), values)
    return jnp.where(turn // 2 % 2 == 1, jnp.flip(values, 3), values)

def faces_from_frame(values, turn):
    turn = turn[None, :, None, None]
    values = jnp.where(turn % 2 == 1, jnp.flip(values, 2), values)
    values = jnp.where(turn // 2 % 2 == 1, jnp.flip(values, 3), values)
    return jnp.where(turn // 4 % 2 == 1, jnp.swapaxes(values, 2, 3), values)

def flip_edges(values, turn):
    return jnp.where(turn[None, :, None] % 2 == 1, jnp.flip(values, 2), values)

def face_frame(slot):
    tangents = [axis for axis in range(3) if slot[axis] == 0]
    edge_list = []
    for axis in tangents:
        for sign in (-1, 1):
            corner = list(slot)
            corner[axis] = sign
            edge_list.append(EDGE_SLOTS.index(tuple(corner)))
    vertex_list = []
    for first in (-1, 1):
        for second in (-1, 1):
            corner = list(slot)
            corner[tangents[0]] = first
            corner[tangents[1]] = second
            vertex_list.append(VERTEX_SLOTS.index(tuple(corner)))
    return (edge_list, vertex_list)

def edge_ends(slot):
    axis = slot.index(0)
    start = list(slot)
    start[axis] = -1
    finish_point = list(slot)
    finish_point[axis] = 1
    return (VERTEX_SLOTS.index(tuple(start)), VERTEX_SLOTS.index(tuple(finish_point)))

def hartley(rows, columns, size):
    phase = rows[:, None] * columns[None, :] % size
    angle = 2.0 * math.pi / size * phase.astype(jnp.float32)
    return (jnp.cos(angle) + jnp.sin(angle)) / math.sqrt(size)

def circle_modes(indices, size):
    return 2.0 - 2.0 * jnp.cos(2.0 * math.pi / size * indices.astype(jnp.float32))

def level_solve(rhs, modes, element_heights):
    inverse = 1.0 / element_heights
    zero = jnp.zeros((1,), jnp.float32)
    stiff = jnp.concatenate([inverse, zero]) + jnp.concatenate([zero, inverse])
    mass = 0.5 * (jnp.concatenate([element_heights, zero]) + jnp.concatenate([zero, element_heights]))
    count = rhs.shape[0]
    primes = []
    values = []
    for level in range(count):
        diagonal = stiff[level] + modes * mass[level]
        if level == 0:
            pivot = diagonal
            value = rhs[0] / pivot
        else:
            pivot = diagonal + inverse[level - 1] * primes[-1]
            value = (rhs[level] + inverse[level - 1] * values[-1]) / pivot
        values.append(value)
        if level < count - 1:
            primes.append(-inverse[level] / pivot)
    solution = [values[-1]]
    for level in range(count - 2, -1, -1):
        solution.append(values[level] - primes[level] * solution[-1])
    return jnp.stack(solution[::-1], axis=0)

def spectral_solve(rhs, element_heights):
    span_x = rhs.shape[1]
    span_z = rhs.shape[2]
    index_x = jnp.arange(span_x, dtype=jnp.int32)
    index_z = jnp.arange(span_z, dtype=jnp.int32)
    spectrum = jnp.einsum('kx,sxzl->skzl', hartley(index_x, index_x, span_x), rhs, precision=HIGHEST)
    spectrum = jnp.einsum('mz,skzl->skml', hartley(index_z, index_z, span_z), spectrum, precision=HIGHEST)
    modes = circle_modes(index_x, span_x)[:, None] + circle_modes(index_z, span_z)[None, :] + shift_mass
    solved = level_solve(jnp.moveaxis(spectrum, 3, 0), modes, element_heights)
    return jnp.moveaxis(solved, 0, 3)

def finish(face_sums, face_cover, edge_sums, edge_cover, extended, face_turn, edge_turn, face_basis, face_eigs, extension, edge_diag):
    solves = face_sums.shape[0]
    nodes = face_basis.shape[0]
    size_x, size_z, layers = face_sums.shape[-3:]
    vertex_values = []
    for slot in VERTEX_SLOTS:
        low_x, low_z, low_y = [(part + 1) // 2 for part in slot]
        vertex_values.append(extended[:, low_x:low_x + size_x, low_z:low_z + size_z, low_y:low_y + layers])
    vertex_values = jnp.stack(vertex_values, axis=1)
    fraction = (jnp.arange(nodes, dtype=jnp.float32) + 1.0) / (nodes + 1.0)
    fraction = fraction[:, None, None, None]
    edge_values = []
    for index, slot in enumerate(EDGE_SLOTS):
        start, stop = edge_ends(slot)
        local = edge_sums[:, index] / (edge_diag[:, None, None, None] * edge_cover[index])
        edge_values.append(local + (1.0 - fraction) * vertex_values[:, start][:, None] + fraction * vertex_values[:, stop][:, None])
    edge_values = jnp.stack(edge_values, axis=1)
    modal = jnp.einsum('ai,sfabxzy->sfibxzy', face_basis, face_sums, precision=HIGHEST)
    modal = jnp.einsum('bj,sfibxzy->sfijxzy', face_basis, modal, precision=HIGHEST)
    spectrum = face_eigs[:, None] + face_eigs[None, :]
    modal = modal / (spectrum[None, None, :, :, None, None, None] * face_cover[None, :, None, None])
    direct = jnp.einsum('ai,sfijxzy->sfajxzy', face_basis, modal, precision=HIGHEST)
    direct = jnp.einsum('bj,sfajxzy->sfabxzy', face_basis, direct, precision=HIGHEST)
    lifted = []
    for slot in FACE_SLOTS:
        edge_list, vertex_list = face_frame(slot)
        boundary = jnp.concatenate([edge_values[:, item] for item in edge_list] + [jnp.stack([vertex_values[:, item] for item in vertex_list], axis=1)], axis=1)
        lifted.append(jnp.einsum('qk,skxzy->sqxzy', extension, boundary, precision=HIGHEST))
    lifted = jnp.stack(lifted, axis=1).reshape((solves, 6, nodes, nodes, size_x, size_z, layers))
    face_values = direct + lifted
    face_out = faces_from_frame(face_values, face_turn).reshape((solves, 6, nodes * nodes, size_x, size_z * layers))
    edge_out = flip_edges(edge_values, edge_turn).reshape((solves, 12, nodes, size_x, size_z * layers))
    vertex_out = vertex_values.reshape((solves, 8, size_x, size_z * layers))
    return (face_out, edge_out, vertex_out)

def reference(face_residual, edge_residual, vertex_residual, face_orient, edge_orient, stiffness, face_basis, face_eigs, extension, edge_diag, element_heights):
    grid = (SPAN_X, SPAN_Z, LAYERS)
    face_turn = face_orient.reshape((6,) + grid)
    edge_turn = edge_orient.reshape((12,) + grid)
    faces = faces_to_frame(face_residual.reshape((SOLVES, 6, NODES, NODES) + grid), face_turn)
    edges = flip_edges(edge_residual.reshape((SOLVES, 12, NODES) + grid), edge_turn)
    corners = vertex_residual.reshape((SOLVES, 8) + grid)
    weight = stiffness.reshape(grid)

    def moved(array, move):
        return shift_levels(jnp.roll(array, (-move[0], -move[1]), axis=(-3, -2)), move[2])

    def face_fetch(index, move):
        return moved(faces[:, index], move)

    def edge_fetch(index, move):
        return moved(edges[:, index], move)

    def vertex_fetch(index, move):
        return moved(corners[:, index], move)

    def weight_fetch(index, move):
        return moved(weight, move)
    face_sums = jnp.stack(sum_slots(FACE_SLOTS, face_fetch), axis=1)
    edge_sums = jnp.stack(sum_slots(EDGE_SLOTS, edge_fetch), axis=1)
    vertex_sums = jnp.stack(sum_slots(VERTEX_SLOTS, vertex_fetch), axis=1)
    edge_cover = jnp.stack(sum_slots(EDGE_SLOTS, weight_fetch), axis=0)
    face_cover = jnp.stack(sum_slots(FACE_SLOTS, weight_fetch), axis=0)
    coarse_rhs = jnp.concatenate([vertex_sums[:, 0], vertex_sums[:, 1][..., -1:]], axis=-1)
    solved = spectral_solve(coarse_rhs, element_heights)
    index_x = jnp.arange(SPAN_X, dtype=jnp.int32)
    index_z = jnp.arange(SPAN_Z, dtype=jnp.int32)
    back = jnp.einsum('xk,skml->sxml', hartley(index_x, index_x, SPAN_X), solved, precision=HIGHEST)
    coarse = jnp.einsum('zm,sxml->sxzl', hartley(index_z, index_z, SPAN_Z), back, precision=HIGHEST)
    extended = jnp.concatenate([coarse, coarse[:, :1]], axis=1)
    extended = jnp.concatenate([extended, extended[:, :, :1]], axis=2)
    return finish(face_sums, face_cover, edge_sums, edge_cover, extended, face_turn, edge_turn, face_basis, face_eigs, extension, edge_diag)
```

```python
import math

import jax
import jax.numpy as jnp
import numpy as np
from jax import lax
from jax.experimental import pallas as pl
from jax.experimental.pallas import tpu as pltpu
from jax.sharding import PartitionSpec as P

F32 = jnp.float32
BF16 = jnp.bfloat16
HIGHEST = lax.Precision.HIGHEST
SHIFT_MASS = 0.004
NX, NZ, LAYERS, LEVELS, NODES = 16, 64, 32, 33, 11
SPLIT_X, SPLIT_Z, OWN_Z = 16, 8, 8
FACE_NODES = 121
EDGE_ROWS = 16 * 12
SIDE_ROWS = 192
VMEM_LIMIT = 40 * 1024 * 1024

FACE_SLOTS = ((-1, 0, 0), (1, 0, 0), (0, -1, 0), (0, 1, 0), (0, 0, -1), (0, 0, 1))
EDGE_SLOTS = (
    (0, -1, -1), (0, -1, 1), (0, 1, -1), (0, 1, 1),
    (-1, 0, -1), (-1, 0, 1), (1, 0, -1), (1, 0, 1),
    (-1, -1, 0), (-1, 1, 0), (1, -1, 0), (1, 1, 0),
)
VERTEX_SLOTS = tuple((x, z, y) for x in (-1, 1) for z in (-1, 1) for y in (-1, 1))
SENT_XP, SENT_XM = (6, 7, 10, 11), (4, 5, 8, 9)
SENT_ZP, SENT_ZM = (2, 3, 9, 11), (0, 1, 8, 10)


def orbits():
    seen, result = set(), []
    last = NODES - 1
    for a in range(NODES):
        for b in range(NODES):
            if (a, b) in seen:
                continue
            group, queue = [], [(a, b)]
            while queue:
                node = queue.pop()
                if node in seen:
                    continue
                seen.add(node)
                group.append(node)
                p, q = node
                queue += [(q, p), (last - p, q), (p, last - q)]
            result.append(group)
    return result


ORBITS = orbits()


def face_frame(slot):
    tangents = [axis for axis in range(3) if slot[axis] == 0]
    edges, corners = [], []
    for axis in tangents:
        for sign in (-1, 1):
            corner = list(slot)
            corner[axis] = sign
            edges.append(EDGE_SLOTS.index(tuple(corner)))
    for first in (-1, 1):
        for second in (-1, 1):
            corner = list(slot)
            corner[tangents[0]] = first
            corner[tangents[1]] = second
            corners.append(VERTEX_SLOTS.index(tuple(corner)))
    return edges, corners


def edge_ends(slot):
    axis = slot.index(0)
    ends = []
    for sign in (-1, 1):
        point = list(slot)
        point[axis] = sign
        ends.append(VERTEX_SLOTS.index(tuple(point)))
    return ends


def hartley_table(size):
    phase = np.outer(np.arange(size), np.arange(size)) % size
    angle = 2.0 * np.pi / size * phase
    return (np.cos(angle) + np.sin(angle)) / math.sqrt(size)


HX, HZ = hartley_table(NX), hartley_table(NZ)


def build_tables():
    f32 = lambda a: np.ascontiguousarray(a, dtype=np.float32)
    tables = {}
    forward = np.zeros((NZ, 128))
    top_a, top_b = np.zeros((128, NZ)), np.zeros((128, NZ))
    for gz in range(SPLIT_Z):
        for kk in range(9):
            column = HZ[:, (8 * gz + kk) % NZ]
            forward[:, gz * 16 + kk] = column
            if kk < 7:
                top_a[gz * 16 + 9 + kk] = column
            else:
                top_b[gz * 16 + 2 + kk] = column
    tables["forward"] = f32(forward)
    tables["top_z"] = f32(np.concatenate([top_a, top_a, top_b, top_b], axis=1))
    lane = np.arange(128)
    lane_s, lane_bx, lane_j = lane // 64, lane // 32 % 2, lane % 32
    mix = np.zeros((NX * NX, 128))
    for k in range(NX):
        for x in range(NX):
            mix[k * NX + x] = HX[k, (x + lane_bx) % NX]
    tables["mix"] = f32(mix)
    top_x = np.zeros((2, 16, 128))
    modes = np.zeros((16, 128))
    waves_x = 2.0 - 2.0 * np.cos(2.0 * np.pi / NX * np.arange(NX))
    waves_z = 2.0 - 2.0 * np.cos(2.0 * np.pi / NZ * np.arange(NZ))
    for row in range(16):
        s, blk, par = row // 8, row // 2 % 4, row % 2
        for pair in range(2):
            k = blk * 4 + pair * 2 + par
            top_x[pair, row] = np.where(lane_s == s, HX[k, (lane_j % 16 + lane_bx) % NX], 0.0)
            modes[row, pair * 64 : pair * 64 + 64] = waves_x[k] + waves_z + SHIFT_MASS
    tables["top_x"] = f32(top_x.reshape(32, 128))
    tables["modes"] = f32(modes)
    back_z = np.zeros((SPLIT_Z, 2, 16, 2, NZ))
    for gz in range(SPLIT_Z):
        for kk in range(9):
            for pair in range(2):
                back_z[gz, pair, kk, pair] = HZ[(8 * gz + kk) % NZ]
    tables["back_z"] = f32(back_z.reshape(SPLIT_Z * 32, 128))
    back_x = np.zeros((SPLIT_X, 2, 4, 2, 2, 64))
    for gx in range(SPLIT_X):
        for bx in range(2):
            for k in range(NX):
                back_x[gx, bx, k // 4, k // 2 % 2, k % 2] = HX[(gx + bx) % NX, k]
    tables["back_x"] = f32(back_x.reshape(SPLIT_X * 16, 128))
    pick = np.zeros((32 + 192, 256))

    def fill(row, s, corner, half):
        bx, bz, by = corner // 4, corner // 2 % 2, corner % 2
        base = (((s * 2 + bx) * 2 + by) * 2 + bz) * 16
        for k in range(4):
            pick[row, base + half * 4 + k + bz] = 1.0

    for s in range(2):
        for half in range(2):
            for corner in range(8):
                fill((s * 8 + corner) * 2 + half, s, corner, half)
            for face, slot in enumerate(FACE_SLOTS):
                for place, corner in enumerate(face_frame(slot)[1]):
                    fill(32 + ((half * 2 + s) * 6 + face) * 8 + place, s, corner, half)
    tables["pick"] = f32(pick)
    expand = np.zeros((2, 128, NODES))
    for q in range(FACE_NODES):
        expand[0, q, q // NODES] = 1.0
        expand[1, q, q % NODES] = 1.0
    tables["rows_a"], tables["rows_b"] = f32(expand[0]), f32(expand[1])
    tables["cols_a"], tables["cols_b"] = f32(expand[0].T), f32(expand[1].T)
    return tables


TABLES = build_tables()


def lanes_of(shape):
    return lax.broadcasted_iota(jnp.int32, shape, 1)


def rows_of(shape):
    return lax.broadcasted_iota(jnp.int32, shape, 0)


def roll(value, shift):
    return pltpu.roll(value, shift % 128, 1)


def every(start, size, stride):
    return pl.ds(start, size, stride=stride)


def from_below(low, high=None):
    lane = lanes_of(low.shape)
    return jnp.where(lane % 32 > 0, roll(low, 1), 0.0)


def from_above(value):
    lane = lanes_of(value.shape)
    return jnp.where(lane % 32 < 31, roll(value, -1), 0.0)


def from_before(pair, halo):
    first, second = roll(pair[0], 32), roll(pair[1], 32)
    head = lanes_of(first.shape) < 32
    return jnp.where(head, halo, first), jnp.where(head, first, second)


def from_after(pair, halo):
    first, second = roll(pair[0], 96), roll(pair[1], 96)
    tail = lanes_of(first.shape) >= 96
    return jnp.where(tail, second, first), jnp.where(tail, halo, second)


def coarse_block(vert, station):
    small = (8, 128)
    lane8, row8 = lanes_of(small), rows_of(small)
    group8 = lane8 // 32
    big = (16, 128)
    lane, row = lanes_of(big), rows_of(big)
    group = lane // 32
    low = [vert[every(half, 8, 4), :] for half in range(2)]
    high = [vert[every(2 + half, 8, 4), :] for half in range(2)]

    def turned(halves):
        parts = []
        for half in range(2):
            for turn in range(4):
                moved = roll(halves[half], 32 * turn)
                for bz in range(2):
                    mask = (group8 == row8 // 2) & (row8 % 2 == bz)
                    total = jnp.sum(jnp.where(mask, moved, 0.0), axis=0, keepdims=True)
                    parts.append((half, turn, bz, jnp.broadcast_to(total, big)))
        return parts

    def spread(parts, point, valid):
        out = jnp.zeros(big, F32)
        for half, turn, bz, total in parts:
            k = point - bz
            mask = (k >= 4 * half) & (k < 4 * half + 4) & (((group - k + 8) % 4) == turn) & valid
            out = out + jnp.where(mask, total, 0.0)
        return out

    main = turned([low[half] + from_below(high[half]) for half in range(2)])
    top = turned(high)
    block = spread(main, row, row < 9)
    last = lane % 32 == 31
    top_a = jnp.where(last, spread(top, row - 9, row >= 9), 0.0)
    top_b = jnp.where(last, spread(top, row - 2, (row >= 9) & (row < 11)), 0.0)
    block = block + pltpu.roll(top_a, station + 97, 1)
    return block + pltpu.roll(top_b, station + 113, 1)


def first_kernel(pos, face, edge, vert, fturn, eturn, stiff, xf, ef, xp, xm, zp, zm, cb):
    block = coarse_block(vert, pos[0])
    for device in range(128):
        cb[device * 16 : device * 16 + 16, :] = block

    last = NODES - 1
    for half in range(2):
        turn = fturn[every(half, 6, 2), :]
        swap, flip_a, flip_b = (turn & 4) != 0, (turn & 1) != 0, (turn & 2) != 0
        for s in range(2):
            source = s * 6 * 242 + half
            target = (half * 2 + s) * 6 * 128
            for group in ORBITS:
                x = {n: face[every(source + 2 * (n[0] * 11 + n[1]), 6, 242), :] for n in group}
                x = {(a, b): jnp.where(swap, x[b, a], x[a, b]) for a, b in group}
                x = {(a, b): jnp.where(flip_a, x[last - a, b], x[a, b]) for a, b in group}
                x = {(a, b): jnp.where(flip_b, x[a, last - b], x[a, b]) for a, b in group}
                for a, b in group:
                    xf[every(target + a * 11 + b, 6, 128), :] = x[a, b]
            for pad in range(121, 128):
                xf[every(target + pad, 6, 128), :] = jnp.zeros((6, 128), F32)
        mirror = eturn[every(half, 12, 2), :] != 0
        for s in range(2):
            source = s * 12 * 22 + half
            target = (half * 2 + s) * EDGE_ROWS
            x = [edge[every(source + 2 * p, 12, 22), :] for p in range(NODES)]
            for p in range(NODES):
                ef[every(target + p, 12, 16), :] = jnp.where(mirror, x[last - p], x[p])
            for pad in range(NODES, 16):
                ef[every(target + pad, 12, 16), :] = jnp.zeros((12, 128), F32)

    for half in range(2):
        weight = stiff[half : half + 1, :]
        for s in range(2):
            tile = half * 2 + s
            base = tile * SIDE_ROWS
            for ref, slot, edges in ((xp, 1, SENT_XP), (xm, 0, SENT_XM)):
                ref[base : base + 128, :] = xf[(tile * 6 + slot) * 128 : (tile * 6 + slot + 1) * 128, :]
                ref[base + 127 : base + 128, :] = weight
                for place, e in enumerate(edges):
                    ref[base + 128 + place * 16 : base + 144 + place * 16, :] = ef[
                        (tile * 12 + e) * 16 : (tile * 12 + e + 1) * 16, :
                    ]
    for ref, half, slot, edges in ((zp, 1, 3, SENT_ZP), (zm, 0, 2, SENT_ZM)):
        own = 96 if half else 0
        group = lanes_of((128, 128)) // 32
        faces = [
            roll(xf[((half * 2 + s) * 6 + slot) * 128 : ((half * 2 + s) * 6 + slot + 1) * 128, :],
                 32 * s - own)
            for s in range(2)
        ]
        lines = jnp.concatenate(
            [ef[((half * 2 + s) * 12 + e) * 16 : ((half * 2 + s) * 12 + e + 1) * 16, :]
             for s in range(2) for e in edges],
            axis=0,
        )
        weight = jnp.broadcast_to(roll(stiff[half : half + 1, :], 96 - own), (128, 128))
        out = jnp.where(group == 0, faces[0], faces[1])
        out = jnp.where(group == 2, roll(lines, 64 - own), out)
        ref[...] = jnp.where(group == 3, weight, out)


def corner_kernel(zp, zm, rxm, rxp, out_p, out_m):
    lane, row = lanes_of((128, 128)), rows_of((128, 128))
    group = lane // 32
    for ref, out, half, place in ((zp, out_p, 1, 3), (zm, out_m, 0, 2)):
        own = 96 if half else 0
        out[...] = ref[...]
        for s in range(2):
            base = (half * 2 + s) * SIDE_ROWS + 128 + place * 16
            for third, side in ((2, rxm), (3, rxp)):
                at = s * 64 + third * 16
                moved = roll(side[base : base + 16, :], 64 - own)
                keep = lanes_of((16, 128)) // 32 == 2
                out[at : at + 16, :] += jnp.where(keep, moved, 0.0)
        for r, side in ((1, rxm), (2, rxp)):
            base = half * 2 * SIDE_ROWS + 127
            moved = roll(side[base : base + 1, :], 96 - own)
            out[r : r + 1, :] += jnp.where(lanes_of((1, 128)) >= 96, moved, 0.0)


def parameter_kernel(heights, diag, basis, eigs, ext, modes, rows_a, rows_b, cols_a, cols_b,
                     pivots, carry, back, lift, rdiag, work):
    def dot(x, y):
        return jnp.dot(x, y, precision=HIGHEST, preferred_element_type=F32)

    b = basis[...]
    kron = dot(dot(rows_a[...], b), cols_a[...]) * dot(dot(rows_b[...], b), cols_b[...])
    scale = dot(eigs[...], cols_a[...] + cols_b[...])
    scale = 1.0 / jnp.where(lanes_of((1, 128)) < FACE_NODES, scale, 1.0)
    work[...] = jnp.zeros((256, 128), F32)
    work[0:128, :] = lax.dot_general(
        kron * scale, kron, (((1,), (1,)), ((), ())), precision=HIGHEST,
        preferred_element_type=F32,
    )
    for place in range(4):
        work[128 + 16 * place : 139 + 16 * place, 0:FACE_NODES] = ext[11 * place : 11 * place + 11, :]
    work[192:196, 0:FACE_NODES] = ext[44:48, :]
    full = work[...].T
    high = full.astype(BF16)
    lift[0:128, :] = high
    lift[128:256, :] = (full - high.astype(F32)).astype(BF16)
    row = rows_of((16, 128))
    nodes = jnp.ones((16, 128), F32)
    for p in range(NODES):
        nodes = jnp.where(row == p, diag[0, p], nodes)
    rdiag[...] = 1.0 / nodes

    wave = modes[...]
    tall = [jnp.full((16, 128), heights[0, l], F32) for l in range(LAYERS)]
    inverse = [1.0 / h for h in tall]
    prime = None
    for l in range(LEVELS):
        if l == 0:
            stiff, mass = inverse[0], 0.5 * tall[0]
        elif l == LAYERS:
            stiff, mass = inverse[l - 1], 0.5 * tall[l - 1]
        else:
            stiff, mass = inverse[l - 1] + inverse[l], 0.5 * (tall[l - 1] + tall[l])
        pivot = stiff + wave * mass
        if l:
            pivot = pivot - inverse[l - 1] * prime
        rp = 1.0 / pivot
        pivots[l * 16 : l * 16 + 16, :] = rp
        if l:
            carry[l * 16 : l * 16 + 16, :] = inverse[l - 1] * rp
        else:
            carry[0:16, :] = jnp.zeros((16, 128), F32)
        if l < LAYERS:
            prime = inverse[l] * rp
            back[l * 16 : l * 16 + 16, :] = prime


def solve_kernel(pos, g, pivots, carry, back, forward, mix, top_z, top_x, back_z, back_x, pick,
                 v_out, vb_out, tz, px, zs, vs, ss, cs):
    def dot(x, y):
        return jnp.dot(x, y, precision=HIGHEST, preferred_element_type=F32)

    stations = [g[x * 128 : x * 128 + 128, :] for x in range(NX)]
    tz[...] = dot(forward[...], jnp.concatenate(stations, axis=1))
    total = g[0:128, :]
    for x in range(1, NX):
        total = total + g[x * 128 : x * 128 + 128, :]
    tops = dot(total.T, top_z[...])
    low = rows_of((128, 128)) % 32 < 16
    tops = jnp.where(low, tops[:, 0:128], tops[:, 128:256])
    tops = dot(top_x[...], tops)
    top = jnp.where(lanes_of((16, 128)) < 64, tops[0:16], tops[16:32])

    bx0 = lanes_of((16, 128)) // 32 % 2 == 0
    for m in range(4):
        t = [tz[m * 16 : m * 16 + 16, x * 128 : x * 128 + 128] for x in range(NX)]
        for kp in range(8):
            pair = []
            for par in range(2):
                k = kp * 2 + par
                acc = t[0] * mix[k * NX : k * NX + 1, :]
                for x in range(1, NX):
                    acc = acc + t[x] * mix[k * NX + x : k * NX + x + 1, :]
                pair.append(acc)
            even, odd = pair
            px[kp * 64 + m * 16 : kp * 64 + m * 16 + 16, :] = jnp.where(
                bx0, even + roll(even, 96), odd + roll(odd, 32)
            )
    for blk in range(4):
        turned = px[blk * 128 : blk * 128 + 128, :].T
        zs[blk * 64 : blk * 64 + 64, :] = turned[0:64]
        zs[256 + blk * 64 : 320 + blk * 64, :] = turned[64:128]

    value = None
    for l in range(LEVELS):
        rhs = zs[every(l, 16, 32), :] if l < LAYERS else top
        at = slice(l * 16, l * 16 + 16)
        value = rhs * pivots[at, :] if l == 0 else rhs * pivots[at, :] + carry[at, :] * value
        vs[at, :] = value
    ss[...] = jnp.zeros((1024, 128), F32)
    for l in range(LEVELS - 1, -1, -1):
        if l < LEVELS - 1:
            at = slice(l * 16, l * 16 + 16)
            value = vs[at, :] + back[at, :] * value
        ss[every(l, 16, 64), :] = value

    hz = back_z[pl.ds(pl.multiple_of(pos[1] * 32, 32), 32), :]
    q = lax.dot_general(hz, ss[...], (((1,), (1,)), ((), ())), precision=HIGHEST,
                        preferred_element_type=F32)
    hx = back_x[pl.ds(pl.multiple_of(pos[0] * 16, 16), 16), :]
    lane, row = lanes_of((16, 128)), rows_of((16, 128))
    group = lane // 32
    for s in range(2):
        for bx in range(2):
            acc = None
            for blk in range(4):
                for pair in range(2):
                    r = (bx * 4 + blk) * 2 + pair
                    term = q[pair * 16 : pair * 16 + 16, (s * 4 + blk) * 128 : (s * 4 + blk + 1) * 128]
                    term = term * hx[r : r + 1, :]
                    acc = term if acc is None else acc + term
            acc = acc + roll(acc, 64)
            for by in range(2):
                plain = roll(acc, 127) if by else acc
                moved = roll(plain, 32)
                mixed = jnp.where(group % 2 == 1, moved, plain)
                for bz in range(2):
                    base = (((s * 2 + bx) * 2 + by) * 2 + bz) * 16
                    keep = (row - bz + 4) % 4 == group
                    cs[base : base + 16, :] = jnp.where(keep, mixed, 0.0)
    picked = dot(pick[...], cs[...])
    v_out[...] = picked[0:32]
    vb_out[...] = picked[32:224]


def final_kernel(xf, ef, rxm, rxp, rzm, rzp, stiff, v, vb, lift, rdiag, fturn, eturn,
                 face_out, edge_out, oq, ev):
    last = NODES - 1
    w = [stiff[half : half + 1, :] for half in range(2)]

    def tile(half, s, f):
        at = ((half * 2 + s) * 6 + f) * 128
        return xf[at : at + 128, :]

    def line(half, s, e):
        at = ((half * 2 + s) * 12 + e) * 16
        return ef[at : at + 16, :]

    def side_face(ref, half, s):
        at = (half * 2 + s) * SIDE_ROWS
        return ref[at : at + 128, :]

    def side_line(ref, half, s, place):
        at = (half * 2 + s) * SIDE_ROWS + 128 + place * 16
        return ref[at : at + 16, :]

    def side_weight(ref, half):
        at = half * 2 * SIDE_ROWS + 127
        return ref[at : at + 1, :]

    def halo_line(ref, s, place, to):
        at = s * 64 + place * 16
        return roll(ref[at : at + 16, :], to - 64)

    wxm = [w[half] + side_weight(rxm, half) for half in range(2)]
    wxp = [w[half] + side_weight(rxp, half) for half in range(2)]
    wzm_in = [roll(rzm[r : r + 1, :], 32) for r in range(3)]
    wzp_in = [rzp[r : r + 1, :] for r in range(3)]

    def add_before(pair, halo):
        moved = from_before(pair, halo)
        return [pair[0] + moved[0], pair[1] + moved[1]]

    def add_after(pair, halo):
        moved = from_after(pair, halo)
        return [pair[0] + moved[0], pair[1] + moved[1]]

    wzm, wzp = add_before(w, wzm_in[0]), add_after(w, wzp_in[0])
    corner = [add_before(wxm, wzm_in[1]), add_after(wxm, wzp_in[1]),
              add_before(wxp, wzm_in[2]), add_after(wxp, wzp_in[2])]
    below = lambda pair: [x + from_below(x) for x in pair]
    above = lambda pair: [x + from_above(x) for x in pair]
    covers = [below(wzm), above(wzm), below(wzp), above(wzp),
              below(wxm), above(wxm), below(wxp), above(wxp)] + corner
    face_covers = [wxm, wxp, wzm, wzp, below(w), above(w)]
    rec_face = [[1.0 / x for x in pair] for pair in face_covers]
    rec_edge = [[1.0 / x for x in pair] for pair in covers]

    row16 = rows_of((16, 128))
    high_t = (row16 + 1).astype(F32) / (NODES + 1.0)
    low_t = 1.0 - high_t
    diag = rdiag[...]

    for s in range(2):
        e = {}
        for half in range(2):
            for k in range(4):
                e[k, half] = line(half, s, k)
            for k, place in ((4, 0), (5, 1), (8, 2), (9, 3)):
                e[k, half] = line(half, s, k) + side_line(rxm, half, s, place)
            for k, place in ((6, 0), (7, 1), (10, 2), (11, 3)):
                e[k, half] = line(half, s, k) + side_line(rxp, half, s, place)
        both = lambda k: (e[k, 0], e[k, 1])
        sums = {}
        for k, other, place in ((0, 2, 0), (1, 3, 1), (8, 9, 2), (10, 11, 3)):
            moved = from_before(both(other), halo_line(rzm, s, place, 0))
            for half in range(2):
                sums[k, half] = e[k, half] + moved[half]
        for k, other, place in ((2, 0, 0), (3, 1, 1), (9, 8, 2), (11, 10, 3)):
            moved = from_after(both(other), halo_line(rzp, s, place, 96))
            for half in range(2):
                sums[k, half] = e[k, half] + moved[half]
        for k in range(4, 8):
            for half in range(2):
                sums[k, half] = e[k, half]
        for half in range(2):
            for k in range(0, 8, 2):
                a, b = sums[k, half], sums[k + 1, half]
                sums[k, half], sums[k + 1, half] = a + from_below(b), b + from_above(a)
            tilebase = (half * 2 + s) * EDGE_ROWS
            vertex = v[every(s * 16 + half, 8, 2), :]
            for k in range(12):
                start, stop = edge_ends(EDGE_SLOTS[k])
                local = sums[k, half] * (diag * rec_edge[k][half])
                ev[tilebase + k * 16 : tilebase + k * 16 + 16, :] = (
                    local + low_t * vertex[start : start + 1] + high_t * vertex[stop : stop + 1]
                )
        for half in range(2):
            columns = []
            for f in range(6):
                own = tile(half, s, f)
                if f == 0:
                    total = own + side_face(rxm, half, s)
                elif f == 1:
                    total = own + side_face(rxp, half, s)
                elif f == 2:
                    halo = roll(rzm[...], -32 * s)
                    total = own + from_before((tile(0, s, 3), tile(1, s, 3)), halo)[half]
                elif f == 3:
                    halo = roll(rzp[...], 96 - 32 * s)
                    total = own + from_after((tile(0, s, 2), tile(1, s, 2)), halo)[half]
                elif f == 4:
                    total = own + from_below(tile(half, s, 5))
                else:
                    total = own + from_above(tile(half, s, 4))
                edges = face_frame(FACE_SLOTS[f])[0]
                tilebase = (half * 2 + s) * EDGE_ROWS
                at = ((half * 2 + s) * 6 + f) * 8
                columns.append(jnp.concatenate(
                    [total * rec_face[f][half]]
                    + [ev[tilebase + k * 16 : tilebase + k * 16 + 16, :] for k in edges]
                    + [vb[at : at + 8, :], jnp.zeros((56, 128), F32)], axis=0))
            full = jnp.concatenate(columns, axis=1)
            high = full.astype(BF16)
            rest = (full - high.astype(F32)).astype(BF16)
            main = jnp.dot(lift[...], high, preferred_element_type=F32)
            more = jnp.dot(lift[0:128, :], rest, preferred_element_type=F32)
            done = main[0:128] + (main[128:256] + more)
            for f in range(6):
                at = ((half * 2 + s) * 6 + f) * 128
                oq[at : at + 128, :] = done[:, f * 128 : f * 128 + 128]

    for half in range(2):
        turn = fturn[every(half, 6, 2), :]
        swap, flip_a, flip_b = (turn & 4) != 0, (turn & 1) != 0, (turn & 2) != 0
        mirror = eturn[every(half, 12, 2), :] != 0
        for s in range(2):
            target = s * 6 * 242 + half
            source = (half * 2 + s) * 6 * 128
            for group in ORBITS:
                x = {n: oq[every(source + n[0] * 11 + n[1], 6, 128), :] for n in group}
                x = {(a, b): jnp.where(flip_a, x[last - a, b], x[a, b]) for a, b in group}
                x = {(a, b): jnp.where(flip_b, x[a, last - b], x[a, b]) for a, b in group}
                x = {(a, b): jnp.where(swap, x[b, a], x[a, b]) for a, b in group}
                for a, b in group:
                    face_out[every(target + 2 * (a * 11 + b), 6, 242), :] = x[a, b]
            target = s * 12 * 22 + half
            source = (half * 2 + s) * EDGE_ROWS
            x = [ev[every(source + p, 12, 16), :] for p in range(NODES)]
            for p in range(NODES):
                edge_out[every(target + 2 * p, 12, 22), :] = jnp.where(mirror, x[last - p], x[p])


VMEM = pl.BlockSpec(memory_space=pltpu.VMEM)
SMEM = pl.BlockSpec(memory_space=pltpu.SMEM)


def call(kernel, outs, args, scalars=0, scratch=(), flops=0, name=None):
    shapes = [jax.ShapeDtypeStruct(o, F32) if isinstance(o, tuple) else o for o in outs]
    size = sum(int(np.prod(a.shape)) * 4 for a in args)
    return pl.pallas_call(
        kernel,
        out_shape=shapes,
        in_specs=[SMEM] * scalars + [VMEM] * (len(args) - scalars),
        out_specs=[VMEM] * len(shapes),
        scratch_shapes=[pltpu.VMEM(o, F32) for o in scratch],
        compiler_params=pltpu.CompilerParams(vmem_limit_bytes=VMEM_LIMIT),
        cost_estimate=pl.CostEstimate(flops=flops, bytes_accessed=size, transcendentals=0),
        name=name,
    )(*args)


def per_device(face_residual, edge_residual, vertex_residual, face_orient, edge_orient, stiffness,
               face_basis, face_eigs, extension, edge_diag, element_heights):
    table = {key: jnp.asarray(value) for key, value in TABLES.items()}
    pos = jnp.stack([lax.axis_index("gx"), lax.axis_index("gz")]).astype(jnp.int32)
    face = face_residual.reshape(2 * 6 * 121 * 2, 128)
    edge = edge_residual.reshape(2 * 12 * 11 * 2, 128)
    vert = vertex_residual.reshape(32, 128)
    fturn = face_orient.reshape(12, 128)
    eturn = edge_orient.reshape(24, 128)
    stiff = stiffness.reshape(2, 128)
    tiles = 24 * 128
    xf, ef, xp, xm, zp, zm, cb = call(
        first_kernel,
        [(tiles, 128), (4 * EDGE_ROWS, 128), (4 * SIDE_ROWS, 128), (4 * SIDE_ROWS, 128),
         (128, 128), (128, 128), (2048, 128)],
        (pos, face, edge, vert, fturn, eturn, stiff), scalars=1, name="frame")
    up = lambda n: [(i, (i + 1) % n) for i in range(n)]
    down = lambda n: [((i + 1) % n, i) for i in range(n)]
    rxm = lax.ppermute(xp, "gx", up(SPLIT_X))
    rxp = lax.ppermute(xm, "gx", down(SPLIT_X))
    pivots, carry, back, lift, rdiag = call(
        parameter_kernel,
        [(LEVELS * 16, 128), (LEVELS * 16, 128), (LAYERS * 16, 128),
         jax.ShapeDtypeStruct((256, 256), BF16), (16, 128)],
        (element_heights.reshape(1, LAYERS), edge_diag.reshape(1, NODES), face_basis,
         face_eigs.reshape(1, NODES), extension.T, table["modes"], table["rows_a"],
         table["rows_b"], table["cols_a"], table["cols_b"]),
        scalars=2, scratch=((256, 128),), name="parameters")
    g = lax.all_to_all(cb.reshape(128, 16, 128), ("gx", "gz"), 0, 0).reshape(2048, 128)
    zp, zm = call(corner_kernel, [(128, 128), (128, 128)], (zp, zm, rxm, rxp), name="corners")
    rzm = lax.ppermute(zp, "gz", up(SPLIT_Z))
    rzp = lax.ppermute(zm, "gz", down(SPLIT_Z))
    v, vb = call(
        solve_kernel, [(32, 128), (192, 128)],
        (pos, g, pivots, carry, back) + tuple(table[k] for k in (
            "forward", "mix", "top_z", "top_x", "back_z", "back_x", "pick")),
        scalars=1,
        scratch=((64, 2048), (512, 128), (512, 128), (LEVELS * 16, 128), (1024, 128), (256, 128)),
        flops=200_000_000, name="coarse")
    face_out, edge_out = call(
        final_kernel, [(2904, 128), (528, 128)],
        (xf, ef, rxm, rxp, rzm, rzp, stiff, v, vb, lift, rdiag, fturn, eturn),
        scratch=((tiles, 128), (4 * EDGE_ROWS, 128)), name="finish")
    return (face_out.reshape(face_residual.shape), edge_out.reshape(edge_residual.shape),
            v.reshape(vertex_residual.shape))


def solution(mesh):
    columns = P(None, None, None, "gx", "gz")
    placed = (columns, columns, P(None, None, "gx", "gz"), P(None, "gx", "gz"),
              P(None, "gx", "gz"), P("gx", "gz"), P(), P(), P(), P(), P())
    return jax.shard_map(
        per_device, mesh=mesh, in_specs=placed,
        out_specs=(columns, columns, P(None, None, "gx", "gz")), check_vma=False)
```

```python
import math

import jax
import jax.numpy as jnp
import numpy as np
from jax import lax
from jax.experimental import pallas as pl
from jax.experimental.pallas import tpu as pltpu
from jax.sharding import PartitionSpec as P

F32 = jnp.float32
BF16 = jnp.bfloat16
HIGHEST = lax.Precision.HIGHEST
SHIFT_MASS = 0.004
NX, NZ, LAYERS, LEVELS, NODES = 16, 64, 32, 33, 11
SPLIT_X, SPLIT_Z, OWN_Z = 16, 8, 8
FACE_NODES = 121
EDGE_ROWS = 16 * 12
SIDE_ROWS = 192
VMEM_LIMIT = 24 * 1024 * 1024
CORNER_FLOPS = 100_000_000_000
VMEM_WHOLE = 60 * 1024 * 1024

FACE_SLOTS = ((-1, 0, 0), (1, 0, 0), (0, -1, 0), (0, 1, 0), (0, 0, -1), (0, 0, 1))
EDGE_SLOTS = (
    (0, -1, -1), (0, -1, 1), (0, 1, -1), (0, 1, 1),
    (-1, 0, -1), (-1, 0, 1), (1, 0, -1), (1, 0, 1),
    (-1, -1, 0), (-1, 1, 0), (1, -1, 0), (1, 1, 0),
)
VERTEX_SLOTS = tuple((x, z, y) for x in (-1, 1) for z in (-1, 1) for y in (-1, 1))
SENT_XP, SENT_XM = (6, 7, 10, 11), (4, 5, 8, 9)
SENT_ZP, SENT_ZM = (2, 3, 9, 11), (0, 1, 8, 10)


def orbits():
    seen, result = set(), []
    last = NODES - 1
    for a in range(NODES):
        for b in range(NODES):
            if (a, b) in seen:
                continue
            group, queue = [], [(a, b)]
            while queue:
                node = queue.pop()
                if node in seen:
                    continue
                seen.add(node)
                group.append(node)
                p, q = node
                queue += [(q, p), (last - p, q), (p, last - q)]
            result.append(group)
    return result


ORBITS = orbits()


def face_frame(slot):
    tangents = [axis for axis in range(3) if slot[axis] == 0]
    edges, corners = [], []
    for axis in tangents:
        for sign in (-1, 1):
            corner = list(slot)
            corner[axis] = sign
            edges.append(EDGE_SLOTS.index(tuple(corner)))
    for first in (-1, 1):
        for second in (-1, 1):
            corner = list(slot)
            corner[tangents[0]] = first
            corner[tangents[1]] = second
            corners.append(VERTEX_SLOTS.index(tuple(corner)))
    return edges, corners


def edge_ends(slot):
    axis = slot.index(0)
    ends = []
    for sign in (-1, 1):
        point = list(slot)
        point[axis] = sign
        ends.append(VERTEX_SLOTS.index(tuple(point)))
    return ends


def hartley_table(size):
    phase = np.outer(np.arange(size), np.arange(size)) % size
    angle = 2.0 * np.pi / size * phase
    return (np.cos(angle) + np.sin(angle)) / math.sqrt(size)


HX, HZ = hartley_table(NX), hartley_table(NZ)


def build_tables():
    f32 = lambda a: np.ascontiguousarray(a, dtype=np.float32)
    tables = {}
    forward = np.zeros((NZ, 128))
    top_a, top_b = np.zeros((128, NZ)), np.zeros((128, NZ))
    for gz in range(SPLIT_Z):
        for kk in range(9):
            column = HZ[:, (8 * gz + kk) % NZ]
            forward[:, gz * 16 + kk] = column
            if kk < 7:
                top_a[gz * 16 + 9 + kk] = column
            else:
                top_b[gz * 16 + 2 + kk] = column
    tables["forward"] = f32(forward)
    tables["top_z"] = f32(np.concatenate([top_a, top_a, top_b, top_b], axis=1))
    lane = np.arange(128)
    lane_s, lane_bx, lane_j = lane // 64, lane // 32 % 2, lane % 32
    mix = np.zeros((NX * NX, 128))
    for k in range(NX):
        for x in range(NX):
            mix[k * NX + x] = HX[k, (x + lane_bx) % NX]
    tables["mix"] = f32(mix)
    top_x = np.zeros((2, 16, 128))
    modes = np.zeros((16, 128))
    waves_x = 2.0 - 2.0 * np.cos(2.0 * np.pi / NX * np.arange(NX))
    waves_z = 2.0 - 2.0 * np.cos(2.0 * np.pi / NZ * np.arange(NZ))
    for row in range(16):
        s, blk, par = row // 8, row // 2 % 4, row % 2
        for pair in range(2):
            k = blk * 4 + pair * 2 + par
            top_x[pair, row] = np.where(lane_s == s, HX[k, (lane_j % 16 + lane_bx) % NX], 0.0)
            modes[row, pair * 64 : pair * 64 + 64] = waves_x[k] + waves_z + SHIFT_MASS
    tables["top_x"] = f32(top_x.reshape(32, 128))
    tables["modes"] = f32(modes)
    back_z = np.zeros((SPLIT_Z, 2, 16, 2, NZ))
    for gz in range(SPLIT_Z):
        for kk in range(9):
            for pair in range(2):
                back_z[gz, pair, kk, pair] = HZ[(8 * gz + kk) % NZ]
    tables["back_z"] = f32(back_z.reshape(SPLIT_Z * 32, 128))
    back_x = np.zeros((SPLIT_X, 2, 4, 2, 2, 64))
    for gx in range(SPLIT_X):
        for bx in range(2):
            for k in range(NX):
                back_x[gx, bx, k // 4, k // 2 % 2, k % 2] = HX[(gx + bx) % NX, k]
    tables["back_x"] = f32(back_x.reshape(SPLIT_X * 16, 128))
    pick = np.zeros((32 + 192, 256))

    def fill(row, s, corner, half):
        bx, bz, by = corner // 4, corner // 2 % 2, corner % 2
        base = (((s * 2 + bx) * 2 + by) * 2 + bz) * 16
        for k in range(4):
            pick[row, base + half * 4 + k + bz] = 1.0

    for s in range(2):
        for half in range(2):
            for corner in range(8):
                fill((s * 8 + corner) * 2 + half, s, corner, half)
            for face, slot in enumerate(FACE_SLOTS):
                for place, corner in enumerate(face_frame(slot)[1]):
                    fill(32 + ((half * 2 + s) * 6 + face) * 8 + place, s, corner, half)
    tables["pick"] = f32(pick)
    expand = np.zeros((2, 128, NODES))
    for q in range(FACE_NODES):
        expand[0, q, q // NODES] = 1.0
        expand[1, q, q % NODES] = 1.0
    tables["cols_a"], tables["cols_b"] = f32(expand[0].T), f32(expand[1].T)
    for name in ("top_z", "pick"):
        wide = tables.pop(name)
        tables[name + "_0"], tables[name + "_1"] = f32(wide[:, :128]), f32(wide[:, 128:])
    rows, places, pieces = 0, {}, []
    for name, value in tables.items():
        count = -(-value.shape[0] // 16) * 16
        places[name] = slice(rows, rows + value.shape[0])
        pieces.append(np.pad(value, ((0, count - value.shape[0]), (0, 0))))
        rows += count
    return f32(np.concatenate(pieces, axis=0)), places


TABLE, PLACE = build_tables()
PIVOTS = TABLE.shape[0]
CARRY = PIVOTS + LEVELS * 16
BACK = CARRY + LEVELS * 16
TABLE_ROWS = BACK + LAYERS * 16


def lanes_of(shape):
    return lax.broadcasted_iota(jnp.int32, shape, 1)


def rows_of(shape):
    return lax.broadcasted_iota(jnp.int32, shape, 0)


def roll(value, shift):
    return pltpu.roll(value, shift % 128, 1)


def every(start, size, stride):
    return pl.ds(start, size, stride=stride)


def from_below(low, high=None):
    lane = lanes_of(low.shape)
    return jnp.where(lane % 32 > 0, roll(low, 1), 0.0)


def from_above(value):
    lane = lanes_of(value.shape)
    return jnp.where(lane % 32 < 31, roll(value, -1), 0.0)


def from_before(pair, halo):
    first, second = roll(pair[0], 32), roll(pair[1], 32)
    head = lanes_of(first.shape) < 32
    return jnp.where(head, halo, first), jnp.where(head, first, second)


def from_after(pair, halo):
    first, second = roll(pair[0], 96), roll(pair[1], 96)
    tail = lanes_of(first.shape) >= 96
    return jnp.where(tail, second, first), jnp.where(tail, halo, second)


def coarse_block(vert, station):
    small = (8, 128)
    lane8, row8 = lanes_of(small), rows_of(small)
    group8 = lane8 // 32
    big = (16, 128)
    lane, row = lanes_of(big), rows_of(big)
    group = lane // 32
    low = [vert[every(half, 8, 4), :] for half in range(2)]
    high = [vert[every(2 + half, 8, 4), :] for half in range(2)]

    def turned(halves):
        parts = []
        for half in range(2):
            for turn in range(4):
                moved = roll(halves[half], 32 * turn)
                for bz in range(2):
                    mask = (group8 == row8 // 2) & (row8 % 2 == bz)
                    total = jnp.sum(jnp.where(mask, moved, 0.0), axis=0, keepdims=True)
                    parts.append((half, turn, bz, jnp.broadcast_to(total, big)))
        return parts

    def spread(parts, point, valid):
        out = jnp.zeros(big, F32)
        for half, turn, bz, total in parts:
            k = point - bz
            mask = (k >= 4 * half) & (k < 4 * half + 4) & (((group - k + 8) % 4) == turn) & valid
            out = out + jnp.where(mask, total, 0.0)
        return out

    main = turned([low[half] + from_below(high[half]) for half in range(2)])
    top = turned(high)
    block = spread(main, row, row < 9)
    last = lane % 32 == 31
    top_a = jnp.where(last, spread(top, row - 9, row >= 9), 0.0)
    top_b = jnp.where(last, spread(top, row - 2, (row >= 9) & (row < 11)), 0.0)
    block = block + pltpu.roll(top_a, station + 97, 1)
    return block + pltpu.roll(top_b, station + 113, 1)


def first_kernel(face_in, edge_in, vert_in, fturn_in, eturn_in, stiff_in,
                 xf_out, ef_out, xp_out, xm_out, zp_out, zm_out, cb_out, turns_out, weights_out,
                 xf, ef, xp, xm, zp, zm, cb, turns, weights,
                 face, edge, vert, fturn, sems, out_sems):
    copies = [
        pltpu.make_async_copy(source, target, sems.at[at])
        for at, (source, target) in enumerate((
            (vert_in, vert),
            (fturn_in, fturn),
            (eturn_in, turns.at[16:40]),
            (stiff_in, weights),
            (face_in.at[0:1448], face.at[0:1448]),
            (edge_in, edge),
            (face_in.at[1448:2904], face.at[1448:2904]),
        ))
    ]
    sent = []

    def send(source, target):
        copy = pltpu.make_async_copy(source, target, out_sems.at[len(sent)])
        copy.start()
        sent.append(copy)

    for copy in copies:
        copy.start()
    copies[0].wait()
    block = coarse_block(vert, lax.axis_index("gx"))
    for device in range(128):
        cb[device * 16 : device * 16 + 16, :] = block
    send(cb, cb_out)
    for copy in copies[1:]:
        copy.wait()
    for f in range(6):
        turns[2 * f : 2 * f + 2, :] = fturn[f]
    turns[12:16, :] = jnp.zeros((4, 128), jnp.int32)
    send(turns, turns_out)
    send(weights, weights_out)
    stiff = weights

    last = NODES - 1
    for half in range(2):
        turn = turns[every(half, 6, 2), :]
        swap, flip_a, flip_b = (turn & 4) != 0, (turn & 1) != 0, (turn & 2) != 0
        for s in range(2):
            source = s * 6 * 242 + half
            target = (half * 2 + s) * 6 * 128
            for group in ORBITS:
                x = {n: face[every(source + 2 * (n[0] * 11 + n[1]), 6, 242), :] for n in group}
                x = {(a, b): jnp.where(swap, x[b, a], x[a, b]) for a, b in group}
                x = {(a, b): jnp.where(flip_a, x[last - a, b], x[a, b]) for a, b in group}
                x = {(a, b): jnp.where(flip_b, x[a, last - b], x[a, b]) for a, b in group}
                for a, b in group:
                    xf[every(target + a * 11 + b, 6, 128), :] = x[a, b]
            for pad in range(121, 128):
                xf[every(target + pad, 6, 128), :] = jnp.zeros((6, 128), F32)
        mirror = turns[every(16 + half, 12, 2), :] != 0
        for s in range(2):
            source = s * 12 * 22 + half
            target = (half * 2 + s) * EDGE_ROWS
            x = [edge[every(source + 2 * p, 12, 22), :] for p in range(NODES)]
            for p in range(NODES):
                ef[every(target + p, 12, 16), :] = jnp.where(mirror, x[last - p], x[p])
            for pad in range(NODES, 16):
                ef[every(target + pad, 12, 16), :] = jnp.zeros((12, 128), F32)

    for half in range(2):
        weight = stiff[half : half + 1, :]
        for s in range(2):
            tile = half * 2 + s
            base = tile * SIDE_ROWS
            for ref, slot, edges in ((xp, 1, SENT_XP), (xm, 0, SENT_XM)):
                ref[base : base + 128, :] = xf[(tile * 6 + slot) * 128 : (tile * 6 + slot + 1) * 128, :]
                ref[base + 127 : base + 128, :] = weight
                for place, e in enumerate(edges):
                    ref[base + 128 + place * 16 : base + 144 + place * 16, :] = ef[
                        (tile * 12 + e) * 16 : (tile * 12 + e + 1) * 16, :
                    ]
    send(xp, xp_out)
    send(xm, xm_out)
    send(ef, ef_out)
    send(xf, xf_out)
    for ref, half, slot, edges in ((zp, 1, 3, SENT_ZP), (zm, 0, 2, SENT_ZM)):
        own = 96 if half else 0
        group = lanes_of((128, 128)) // 32
        faces = [
            roll(xf[((half * 2 + s) * 6 + slot) * 128 : ((half * 2 + s) * 6 + slot + 1) * 128, :],
                 32 * s - own)
            for s in range(2)
        ]
        lines = jnp.concatenate(
            [ef[((half * 2 + s) * 12 + e) * 16 : ((half * 2 + s) * 12 + e + 1) * 16, :]
             for s in range(2) for e in edges],
            axis=0,
        )
        weight = jnp.broadcast_to(roll(stiff[half : half + 1, :], 96 - own), (128, 128))
        out = jnp.where(group == 0, faces[0], faces[1])
        out = jnp.where(group == 2, roll(lines, 64 - own), out)
        ref[...] = jnp.where(group == 3, weight, out)
    send(zp, zp_out)
    send(zm, zm_out)
    for copy in sent:
        copy.wait()


def corner_kernel(zp, zm, rxm, rxp, out_p, out_m):
    lane, row = lanes_of((128, 128)), rows_of((128, 128))
    group = lane // 32
    for ref, out, half, place in ((zp, out_p, 1, 3), (zm, out_m, 0, 2)):
        own = 96 if half else 0
        out[...] = ref[...]
        for s in range(2):
            base = (half * 2 + s) * SIDE_ROWS + 128 + place * 16
            for third, side in ((2, rxm), (3, rxp)):
                at = s * 64 + third * 16
                moved = roll(side[base : base + 16, :], 64 - own)
                keep = lanes_of((16, 128)) // 32 == 2
                out[at : at + 16, :] += jnp.where(keep, moved, 0.0)
        for r, side in ((1, rxm), (2, rxp)):
            base = half * 2 * SIDE_ROWS + 127
            moved = roll(side[base : base + 1, :], 96 - own)
            out[r : r + 1, :] += jnp.where(lanes_of((1, 128)) >= 96, moved, 0.0)


def parameter_kernel(table_in, heights_in, diag_in, basis_in, eigs_in, ext_in,
                     table, lift, rdiag, heights, diag, basis, eigs, ext, work, sems):
    copies = [
        pltpu.make_async_copy(source, target, sems.at[at])
        for at, (source, target) in enumerate((
            (heights_in, heights), (diag_in, diag), (basis_in, basis), (eigs_in, eigs),
            (ext_in, ext), (table_in, table.at[0:PIVOTS]),
        ))
    ]
    for copy in copies:
        copy.start()
    for copy in copies:
        copy.wait()

    def dot(x, y):
        return jnp.dot(x, y, precision=HIGHEST, preferred_element_type=F32)

    def dot_first(x, y):
        return lax.dot_general(x, y, (((0,), (0,)), ((), ())), precision=HIGHEST,
                               preferred_element_type=F32)

    b = basis[...]
    cols_a, cols_b = table[PLACE["cols_a"], :], table[PLACE["cols_b"], :]
    modes = table[PLACE["modes"], :]
    kron = dot(dot_first(cols_a, b), cols_a) * dot(dot_first(cols_b, b), cols_b)
    scale = dot(eigs[...], cols_a + cols_b)
    scale = 1.0 / jnp.where(lanes_of((1, 128)) < FACE_NODES, scale, 1.0)
    work[...] = jnp.zeros((256, 128), F32)
    work[0:128, :] = lax.dot_general(
        kron * scale, kron, (((1,), (1,)), ((), ())), precision=HIGHEST,
        preferred_element_type=F32,
    )
    for place in range(4):
        work[128 + 16 * place : 139 + 16 * place, 0:FACE_NODES] = ext[11 * place : 11 * place + 11, :]
    work[192:196, 0:FACE_NODES] = ext[44:48, :]
    full = work[...].T
    high = full.astype(BF16)
    lift[0:128, :] = high
    lift[128:256, :] = (full - high.astype(F32)).astype(BF16)
    row = rows_of((16, 128))
    nodes = jnp.ones((16, 128), F32)
    for p in range(NODES):
        nodes = jnp.where(row == p, diag[0:1, p : p + 1], nodes)
    rdiag[...] = 1.0 / nodes

    wave = modes
    tall = [jnp.broadcast_to(heights[0:1, l : l + 1], (16, 128)) for l in range(LAYERS)]
    inverse = [1.0 / h for h in tall]
    prime = None
    for l in range(LEVELS):
        if l == 0:
            stiff, mass = inverse[0], 0.5 * tall[0]
        elif l == LAYERS:
            stiff, mass = inverse[l - 1], 0.5 * tall[l - 1]
        else:
            stiff, mass = inverse[l - 1] + inverse[l], 0.5 * (tall[l - 1] + tall[l])
        pivot = stiff + wave * mass
        if l:
            pivot = pivot - inverse[l - 1] * prime
        rp = 1.0 / pivot
        table[PIVOTS + l * 16 : PIVOTS + l * 16 + 16, :] = rp
        if l:
            table[CARRY + l * 16 : CARRY + l * 16 + 16, :] = inverse[l - 1] * rp
        else:
            table[CARRY : CARRY + 16, :] = jnp.zeros((16, 128), F32)
        if l < LAYERS:
            prime = inverse[l] * rp
            table[BACK + l * 16 : BACK + l * 16 + 16, :] = prime


def solve_kernel(g, table, v_out, v_hbm, vb_out, tz, px, zs, vs, ss, cs, sem):
    def dot(x, y):
        return jnp.dot(x, y, precision=HIGHEST, preferred_element_type=F32)

    stations = [g[x * 128 : x * 128 + 128, :] for x in range(NX)]
    tz[...] = dot(table[PLACE["forward"], :], jnp.concatenate(stations, axis=1))
    total = g[0:128, :]
    for x in range(1, NX):
        total = total + g[x * 128 : x * 128 + 128, :]
    total = total.T
    low = rows_of((128, 128)) % 32 < 16
    tops = jnp.where(low, dot(total, table[PLACE["top_z_0"], :]),
                     dot(total, table[PLACE["top_z_1"], :]))
    tops = dot(table[PLACE["top_x"], :], tops)
    mix = PLACE["mix"].start
    top = jnp.where(lanes_of((16, 128)) < 64, tops[0:16], tops[16:32])

    bx0 = lanes_of((16, 128)) // 32 % 2 == 0
    for m in range(4):
        t = [tz[m * 16 : m * 16 + 16, x * 128 : x * 128 + 128] for x in range(NX)]
        for kp in range(8):
            pair = []
            for par in range(2):
                k = kp * 2 + par
                acc = t[0] * table[mix + k * NX : mix + k * NX + 1, :]
                for x in range(1, NX):
                    acc = acc + t[x] * table[mix + k * NX + x : mix + k * NX + x + 1, :]
                pair.append(acc)
            even, odd = pair
            px[kp * 64 + m * 16 : kp * 64 + m * 16 + 16, :] = jnp.where(
                bx0, even + roll(even, 96), odd + roll(odd, 32)
            )
    for blk in range(4):
        turned = px[blk * 128 : blk * 128 + 128, :].T
        zs[blk * 64 : blk * 64 + 64, :] = turned[0:64]
        zs[256 + blk * 64 : 320 + blk * 64, :] = turned[64:128]

    value = None
    for l in range(LEVELS):
        rhs = zs[every(l, 16, 32), :] if l < LAYERS else top
        at = l * 16
        step = rhs * table[PIVOTS + at : PIVOTS + at + 16, :]
        value = step if l == 0 else step + table[CARRY + at : CARRY + at + 16, :] * value
        vs[at : at + 16, :] = value
    ss[...] = jnp.zeros((1024, 128), F32)
    for l in range(LEVELS - 1, -1, -1):
        if l < LEVELS - 1:
            at = l * 16
            value = vs[at : at + 16, :] + table[BACK + at : BACK + at + 16, :] * value
        ss[every(l, 16, 64), :] = value

    at = PLACE["back_z"].start + lax.axis_index("gz") * 32
    hz = table[pl.ds(pl.multiple_of(at, 16), 32), :]
    q = lax.dot_general(hz, ss[...], (((1,), (1,)), ((), ())), precision=HIGHEST,
                        preferred_element_type=F32)
    at = PLACE["back_x"].start + lax.axis_index("gx") * 16
    hx = table[pl.ds(pl.multiple_of(at, 16), 16), :]
    lane, row = lanes_of((16, 128)), rows_of((16, 128))
    group = lane // 32
    for s in range(2):
        for bx in range(2):
            acc = None
            for blk in range(4):
                for pair in range(2):
                    r = (bx * 4 + blk) * 2 + pair
                    term = q[pair * 16 : pair * 16 + 16, (s * 4 + blk) * 128 : (s * 4 + blk + 1) * 128]
                    term = term * hx[r : r + 1, :]
                    acc = term if acc is None else acc + term
            acc = acc + roll(acc, 64)
            for by in range(2):
                plain = roll(acc, 127) if by else acc
                moved = roll(plain, 32)
                mixed = jnp.where(group % 2 == 1, moved, plain)
                for bz in range(2):
                    base = (((s * 2 + bx) * 2 + by) * 2 + bz) * 16
                    keep = (row - bz + 4) % 4 == group
                    cs[base : base + 16, :] = jnp.where(keep, mixed, 0.0)
    picked = dot(table[PLACE["pick_0"], :], cs[0:128, :]) + dot(table[PLACE["pick_1"], :], cs[128:256, :])
    v_out[...] = picked[0:32]
    copy = pltpu.make_async_copy(v_out, v_hbm, sem)
    copy.start()
    vb_out[...] = picked[32:224]
    copy.wait()


def final_kernel(xf, ef, rxm, rxp, rzm, rzp, stiff, v, vb, lift, rdiag, turns,
                 face_hbm, edge_hbm, oq, ev, face_out, edge_out, sems):
    last = NODES - 1
    w = [stiff[half : half + 1, :] for half in range(2)]

    def tile(half, s, f):
        at = ((half * 2 + s) * 6 + f) * 128
        return xf[at : at + 128, :]

    def line(half, s, e):
        at = ((half * 2 + s) * 12 + e) * 16
        return ef[at : at + 16, :]

    def side_face(ref, half, s):
        at = (half * 2 + s) * SIDE_ROWS
        return ref[at : at + 128, :]

    def side_line(ref, half, s, place):
        at = (half * 2 + s) * SIDE_ROWS + 128 + place * 16
        return ref[at : at + 16, :]

    def side_weight(ref, half):
        at = half * 2 * SIDE_ROWS + 127
        return ref[at : at + 1, :]

    def halo_line(ref, s, place, to):
        at = s * 64 + place * 16
        return roll(ref[at : at + 16, :], to - 64)

    wxm = [w[half] + side_weight(rxm, half) for half in range(2)]
    wxp = [w[half] + side_weight(rxp, half) for half in range(2)]
    wzm_in = [roll(rzm[r : r + 1, :], 32) for r in range(3)]
    wzp_in = [rzp[r : r + 1, :] for r in range(3)]

    def add_before(pair, halo):
        moved = from_before(pair, halo)
        return [pair[0] + moved[0], pair[1] + moved[1]]

    def add_after(pair, halo):
        moved = from_after(pair, halo)
        return [pair[0] + moved[0], pair[1] + moved[1]]

    wzm, wzp = add_before(w, wzm_in[0]), add_after(w, wzp_in[0])
    corner = [add_before(wxm, wzm_in[1]), add_after(wxm, wzp_in[1]),
              add_before(wxp, wzm_in[2]), add_after(wxp, wzp_in[2])]
    below = lambda pair: [x + from_below(x) for x in pair]
    above = lambda pair: [x + from_above(x) for x in pair]
    covers = [below(wzm), above(wzm), below(wzp), above(wzp),
              below(wxm), above(wxm), below(wxp), above(wxp)] + corner
    face_covers = [wxm, wxp, wzm, wzp, below(w), above(w)]
    rec_face = [[1.0 / x for x in pair] for pair in face_covers]
    rec_edge = [[1.0 / x for x in pair] for pair in covers]

    row16 = rows_of((16, 128))
    high_t = (row16 + 1).astype(F32) / (NODES + 1.0)
    low_t = 1.0 - high_t
    diag = rdiag[...]
    copies = []

    for s in range(2):
        e = {}
        for half in range(2):
            for k in range(4):
                e[k, half] = line(half, s, k)
            for k, place in ((4, 0), (5, 1), (8, 2), (9, 3)):
                e[k, half] = line(half, s, k) + side_line(rxm, half, s, place)
            for k, place in ((6, 0), (7, 1), (10, 2), (11, 3)):
                e[k, half] = line(half, s, k) + side_line(rxp, half, s, place)
        both = lambda k: (e[k, 0], e[k, 1])
        sums = {}
        for k, other, place in ((0, 2, 0), (1, 3, 1), (8, 9, 2), (10, 11, 3)):
            moved = from_before(both(other), halo_line(rzm, s, place, 0))
            for half in range(2):
                sums[k, half] = e[k, half] + moved[half]
        for k, other, place in ((2, 0, 0), (3, 1, 1), (9, 8, 2), (11, 10, 3)):
            moved = from_after(both(other), halo_line(rzp, s, place, 96))
            for half in range(2):
                sums[k, half] = e[k, half] + moved[half]
        for k in range(4, 8):
            for half in range(2):
                sums[k, half] = e[k, half]
        for half in range(2):
            for k in range(0, 8, 2):
                a, b = sums[k, half], sums[k + 1, half]
                sums[k, half], sums[k + 1, half] = a + from_below(b), b + from_above(a)
            tilebase = (half * 2 + s) * EDGE_ROWS
            vertex = v[every(s * 16 + half, 8, 2), :]
            for k in range(12):
                start, stop = edge_ends(EDGE_SLOTS[k])
                local = sums[k, half] * (diag * rec_edge[k][half])
                ev[tilebase + k * 16 : tilebase + k * 16 + 16, :] = (
                    local + low_t * vertex[start : start + 1] + high_t * vertex[stop : stop + 1]
                )
        for half in range(2):
            columns = []
            for f in range(6):
                own = tile(half, s, f)
                if f == 0:
                    total = own + side_face(rxm, half, s)
                elif f == 1:
                    total = own + side_face(rxp, half, s)
                elif f == 2:
                    halo = roll(rzm[...], -32 * s)
                    total = own + from_before((tile(0, s, 3), tile(1, s, 3)), halo)[half]
                elif f == 3:
                    halo = roll(rzp[...], 96 - 32 * s)
                    total = own + from_after((tile(0, s, 2), tile(1, s, 2)), halo)[half]
                elif f == 4:
                    total = own + from_below(tile(half, s, 5))
                else:
                    total = own + from_above(tile(half, s, 4))
                edges = face_frame(FACE_SLOTS[f])[0]
                tilebase = (half * 2 + s) * EDGE_ROWS
                at = ((half * 2 + s) * 6 + f) * 8
                columns.append(jnp.concatenate(
                    [total * rec_face[f][half]]
                    + [ev[tilebase + k * 16 : tilebase + k * 16 + 16, :] for k in edges]
                    + [vb[at : at + 8, :], jnp.zeros((56, 128), F32)], axis=0))
            full = jnp.concatenate(columns, axis=1)
            high = full.astype(BF16)
            rest = (full - high.astype(F32)).astype(BF16)
            main = jnp.dot(lift[...], high, preferred_element_type=F32)
            more = jnp.dot(lift[0:128, :], rest, preferred_element_type=F32)
            done = main[0:128] + (main[128:256] + more)
            for f in range(6):
                at = ((half * 2 + s) * 6 + f) * 128
                oq[at : at + 128, :] = done[:, f * 128 : f * 128 + 128]

        for half in range(2):
            turn = turns[every(half, 6, 2), :]
            swap, flip_a, flip_b = (turn & 4) != 0, (turn & 1) != 0, (turn & 2) != 0
            target = s * 6 * 242 + half
            source = (half * 2 + s) * 6 * 128
            for group in ORBITS:
                x = {n: oq[every(source + n[0] * 11 + n[1], 6, 128), :] for n in group}
                x = {(a, b): jnp.where(flip_a, x[last - a, b], x[a, b]) for a, b in group}
                x = {(a, b): jnp.where(flip_b, x[a, last - b], x[a, b]) for a, b in group}
                x = {(a, b): jnp.where(swap, x[b, a], x[a, b]) for a, b in group}
                for a, b in group:
                    face_out[every(target + 2 * (a * 11 + b), 6, 242), :] = x[a, b]
            mirror = turns[every(16 + half, 12, 2), :] != 0
            target = s * 12 * 22 + half
            source = (half * 2 + s) * EDGE_ROWS
            x = [ev[every(source + p, 12, 16), :] for p in range(NODES)]
            for p in range(NODES):
                edge_out[every(target + 2 * p, 12, 22), :] = jnp.where(mirror, x[last - p], x[p])
        rows = (slice(0, 1448), slice(1448, 2904))[s]
        copies.append(pltpu.make_async_copy(face_out.at[rows], face_hbm.at[rows], sems.at[2 * s]))
        rows = slice(s * 264, s * 264 + 264)
        copies.append(pltpu.make_async_copy(edge_out.at[rows], edge_hbm.at[rows], sems.at[2 * s + 1]))
        for copy in copies[2 * s : 2 * s + 2]:
            copy.start()
    for copy in copies:
        copy.wait()


VMEM = pl.BlockSpec(memory_space=pltpu.VMEM)
HBM = pl.BlockSpec(memory_space=pltpu.HBM)


def call(kernel, name, args, ins, outs, out_specs, scratch=(), sems=(), flops=0,
         limit=VMEM_LIMIT):
    shapes = [jax.ShapeDtypeStruct(o, F32) if isinstance(o, tuple) else o for o in outs]
    held = [pltpu.VMEM(o, F32) if isinstance(o, tuple) else o for o in scratch]
    held += [pltpu.SemaphoreType.DMA(n) for n in sems]
    size = sum(int(np.prod(a.shape)) * 4 for a in args)
    return pl.pallas_call(
        kernel,
        out_shape=shapes,
        in_specs=ins,
        out_specs=out_specs,
        scratch_shapes=held,
        compiler_params=pltpu.CompilerParams(vmem_limit_bytes=limit),
        cost_estimate=pl.CostEstimate(flops=flops, bytes_accessed=size, transcendentals=0),
        name=name,
    )(*args)


def per_device(face_residual, edge_residual, vertex_residual, face_orient, edge_orient, stiffness,
               face_basis, face_eigs, extension, edge_diag, element_heights):
    face = face_residual.reshape(2904, 128)
    edge = edge_residual.reshape(528, 128)
    vert = vertex_residual.reshape(32, 128)
    fturn = face_orient.reshape(6, 2, 128)
    eturn = edge_orient.reshape(24, 128)
    stiff = stiffness.reshape(2, 128)
    tiles = 24 * 128
    kept = [(tiles, 128), (4 * EDGE_ROWS, 128), (4 * SIDE_ROWS, 128), (4 * SIDE_ROWS, 128),
            (128, 128), (128, 128), (2048, 128), (40, 128), (2, 128)]
    kinds = [F32] * 7 + [jnp.int32, F32]
    xf, ef, xp, xm, zp, zm, cb, turns, weights = call(
        first_kernel, "frame", (face, edge, vert, fturn, eturn, stiff), [HBM] * 6,
        [jax.ShapeDtypeStruct(o, kind) for o, kind in zip(kept, kinds)], [HBM] * 9,
        [pltpu.VMEM(o, kind) for o, kind in zip(kept, kinds)]
        + [(2904, 128), (528, 128), (32, 128), pltpu.VMEM((6, 2, 128), jnp.int32)],
        ((7,), (9,)), limit=VMEM_WHOLE)
    up = lambda n: [(i, (i + 1) % n) for i in range(n)]
    down = lambda n: [((i + 1) % n, i) for i in range(n)]
    rxm = lax.ppermute(xp, "gx", up(SPLIT_X))
    rxp = lax.ppermute(xm, "gx", down(SPLIT_X))
    table, lift, rdiag = call(
        parameter_kernel, "parameters",
        (jnp.asarray(TABLE), element_heights.reshape(1, LAYERS), edge_diag.reshape(1, NODES),
         face_basis, face_eigs.reshape(1, NODES), extension.T), [HBM] * 6,
        [(TABLE_ROWS, 128), jax.ShapeDtypeStruct((256, 256), BF16), (16, 128)], [VMEM] * 3,
        ((1, LAYERS), (1, NODES), (NODES, NODES), (1, NODES), (48, FACE_NODES), (256, 128)), ((6,),),
        limit=VMEM_WHOLE)
    g = lax.all_to_all(cb.reshape(128, 16, 128), ("gx", "gz"), 0, 0).reshape(2048, 128)
    zp, zm = call(corner_kernel, "corners", (zp, zm, rxm, rxp), [VMEM] * 4,
                  [(128, 128), (128, 128)], [VMEM] * 2, flops=CORNER_FLOPS)
    rzm = lax.ppermute(zp, "gz", up(SPLIT_Z))
    rzp = lax.ppermute(zm, "gz", down(SPLIT_Z))
    v, v_out, vb = call(
        solve_kernel, "coarse", (g, table), [VMEM] * 2, [(32, 128), (32, 128), (192, 128)],
        [VMEM, HBM, VMEM],
        ((64, 2048), (512, 128), (512, 128), (LEVELS * 16, 128), (1024, 128), (256, 128)), ((),),
        flops=200_000_000)
    face_out, edge_out = call(
        final_kernel, "finish",
        (xf, ef, rxm, rxp, rzm, rzp, weights, v, vb, lift, rdiag, turns), [VMEM] * 12,
        [(2904, 128), (528, 128)], [HBM] * 2,
        ((tiles, 128), (4 * EDGE_ROWS, 128), (2904, 128), (528, 128)), ((4,),))
    return (face_out.reshape(face_residual.shape), edge_out.reshape(edge_residual.shape),
            v_out.reshape(vertex_residual.shape))


def solution(mesh):
    columns = P(None, None, None, "gx", "gz")
    placed = (columns, columns, P(None, None, "gx", "gz"), P(None, "gx", "gz"),
              P(None, "gx", "gz"), P("gx", "gz"), P(), P(), P(), P(), P())
    return jax.shard_map(
        per_device, mesh=mesh, in_specs=placed,
        out_specs=(columns, columns, P(None, None, "gx", "gz")), check_vma=False)
```

```python
import math

import jax
import jax.numpy as jnp
import numpy as np
from jax import lax
from jax.experimental import pallas as pl
from jax.experimental.pallas import tpu as pltpu
from jax.sharding import PartitionSpec as P

F32 = jnp.float32
BF16 = jnp.bfloat16
HIGHEST = lax.Precision.HIGHEST
SHIFT_MASS = 0.004
NX, NZ, LAYERS, LEVELS, NODES = 16, 64, 32, 33, 11
SPLIT_X, SPLIT_Z, OWN_Z = 16, 8, 8
FACE_NODES = 121
EDGE_ROWS = 16 * 12
SIDE_ROWS = 192
SENT = 12
STATION = SENT * SPLIT_Z
VMEM_LIMIT = 24 * 1024 * 1024
CORNER_FLOPS = 100_000_000_000
VMEM_WHOLE = 60 * 1024 * 1024

FACE_SLOTS = ((-1, 0, 0), (1, 0, 0), (0, -1, 0), (0, 1, 0), (0, 0, -1), (0, 0, 1))
EDGE_SLOTS = (
    (0, -1, -1), (0, -1, 1), (0, 1, -1), (0, 1, 1),
    (-1, 0, -1), (-1, 0, 1), (1, 0, -1), (1, 0, 1),
    (-1, -1, 0), (-1, 1, 0), (1, -1, 0), (1, 1, 0),
)
VERTEX_SLOTS = tuple((x, z, y) for x in (-1, 1) for z in (-1, 1) for y in (-1, 1))
SENT_XP, SENT_XM = (6, 7, 10, 11), (4, 5, 8, 9)
SENT_ZP, SENT_ZM = (2, 3, 9, 11), (0, 1, 8, 10)


def orbits():
    seen, result = set(), []
    last = NODES - 1
    for a in range(NODES):
        for b in range(NODES):
            if (a, b) in seen:
                continue
            group, queue = [], [(a, b)]
            while queue:
                node = queue.pop()
                if node in seen:
                    continue
                seen.add(node)
                group.append(node)
                p, q = node
                queue += [(q, p), (last - p, q), (p, last - q)]
            result.append(group)
    return result


ORBITS = orbits()


def face_frame(slot):
    tangents = [axis for axis in range(3) if slot[axis] == 0]
    edges, corners = [], []
    for axis in tangents:
        for sign in (-1, 1):
            corner = list(slot)
            corner[axis] = sign
            edges.append(EDGE_SLOTS.index(tuple(corner)))
    for first in (-1, 1):
        for second in (-1, 1):
            corner = list(slot)
            corner[tangents[0]] = first
            corner[tangents[1]] = second
            corners.append(VERTEX_SLOTS.index(tuple(corner)))
    return edges, corners


def edge_ends(slot):
    axis = slot.index(0)
    ends = []
    for sign in (-1, 1):
        point = list(slot)
        point[axis] = sign
        ends.append(VERTEX_SLOTS.index(tuple(point)))
    return ends


def hartley_table(size):
    phase = np.outer(np.arange(size), np.arange(size)) % size
    angle = 2.0 * np.pi / size * phase
    return (np.cos(angle) + np.sin(angle)) / math.sqrt(size)


HX, HZ = hartley_table(NX), hartley_table(NZ)


def build_tables():
    f32 = lambda a: np.ascontiguousarray(a, dtype=np.float32)
    tables = {}
    forward = np.zeros((NZ, 128))
    top_z = np.zeros((3, 128, 2 * NZ))
    for gz in range(SPLIT_Z):
        for kk in range(9):
            column = HZ[:, (8 * gz + kk) % NZ]
            forward[:, gz * SENT + kk] = column
            top_z[kk // 3, gz * SENT + 9 + kk % 3] = np.tile(column, 2)
    tables["forward"] = f32(forward)
    tables["top_z"] = f32(top_z.reshape(3 * 128, 128))
    lane = np.arange(128)
    lane_s, lane_bx, lane_j = lane // 64, lane // 32 % 2, lane % 32
    mix = np.zeros((NX * NX, 128))
    for k in range(NX):
        for x in range(NX):
            mix[k * NX + x] = HX[k, (x + lane_bx) % NX]
    tables["mix"] = f32(mix)
    top_x = np.zeros((2, 2, 16, 128))
    modes = np.zeros((16, 128))
    waves_x = 2.0 - 2.0 * np.cos(2.0 * np.pi / NX * np.arange(NX))
    waves_z = 2.0 - 2.0 * np.cos(2.0 * np.pi / NZ * np.arange(NZ))
    for row in range(16):
        s, blk, par = row // 8, row // 2 % 4, row % 2
        for pair in range(2):
            k = blk * 4 + pair * 2 + par
            for odd in range(2):
                x = 2 * (lane_j % 8) + odd
                top_x[odd, pair, row] = np.where(lane_s == s, HX[k, (x + lane_bx) % NX], 0.0)
            modes[row, pair * 64 : pair * 64 + 64] = waves_x[k] + waves_z + SHIFT_MASS
    tables["top_x"] = f32(top_x.reshape(64, 128))
    tables["modes"] = f32(modes)
    back_z = np.zeros((SPLIT_Z, 2, 16, 2, NZ))
    for gz in range(SPLIT_Z):
        for kk in range(9):
            for pair in range(2):
                back_z[gz, pair, kk, pair] = HZ[(8 * gz + kk) % NZ]
    tables["back_z"] = f32(back_z.reshape(SPLIT_Z * 32, 128))
    back_x = np.zeros((SPLIT_X, 2, 4, 2, 2, 64))
    for gx in range(SPLIT_X):
        for bx in range(2):
            for k in range(NX):
                back_x[gx, bx, k // 4, k // 2 % 2, k % 2] = HX[(gx + bx) % NX, k]
    tables["back_x"] = f32(back_x.reshape(SPLIT_X * 16, 128))
    pick = np.zeros((32 + 192, 256))

    def fill(row, s, corner, half):
        bx, bz, by = corner // 4, corner // 2 % 2, corner % 2
        base = (((s * 2 + bx) * 2 + by) * 2 + bz) * 16
        for k in range(4):
            pick[row, base + half * 4 + k + bz] = 1.0

    for s in range(2):
        for half in range(2):
            for corner in range(8):
                fill((s * 8 + corner) * 2 + half, s, corner, half)
            for face, slot in enumerate(FACE_SLOTS):
                for place, corner in enumerate(face_frame(slot)[1]):
                    fill(32 + ((half * 2 + s) * 6 + face) * 8 + place, s, corner, half)
    tables["pick"] = f32(pick)
    expand = np.zeros((2, 128, NODES))
    for q in range(FACE_NODES):
        expand[0, q, q // NODES] = 1.0
        expand[1, q, q % NODES] = 1.0
    tables["cols_a"], tables["cols_b"] = f32(expand[0].T), f32(expand[1].T)
    for name in ("pick",):
        wide = tables.pop(name)
        tables[name + "_0"], tables[name + "_1"] = f32(wide[:, :128]), f32(wide[:, 128:])
    rows, places, pieces = 0, {}, []
    for name, value in tables.items():
        count = -(-value.shape[0] // 16) * 16
        places[name] = slice(rows, rows + value.shape[0])
        pieces.append(np.pad(value, ((0, count - value.shape[0]), (0, 0))))
        rows += count
    return f32(np.concatenate(pieces, axis=0)), places


TABLE, PLACE = build_tables()
PIVOTS = TABLE.shape[0]
CARRY = PIVOTS + LEVELS * 16
BACK = CARRY + LEVELS * 16
TABLE_ROWS = BACK + LAYERS * 16


def lanes_of(shape):
    return lax.broadcasted_iota(jnp.int32, shape, 1)


def rows_of(shape):
    return lax.broadcasted_iota(jnp.int32, shape, 0)


def roll(value, shift):
    return pltpu.roll(value, shift % 128, 1)


def every(start, size, stride):
    return pl.ds(start, size, stride=stride)


def from_below(low, high=None):
    lane = lanes_of(low.shape)
    return jnp.where(lane % 32 > 0, roll(low, 1), 0.0)


def from_above(value):
    lane = lanes_of(value.shape)
    return jnp.where(lane % 32 < 31, roll(value, -1), 0.0)


def from_before(pair, halo):
    first, second = roll(pair[0], 32), roll(pair[1], 32)
    head = lanes_of(first.shape) < 32
    return jnp.where(head, halo, first), jnp.where(head, first, second)


def from_after(pair, halo):
    first, second = roll(pair[0], 96), roll(pair[1], 96)
    tail = lanes_of(first.shape) >= 96
    return jnp.where(tail, second, first), jnp.where(tail, halo, second)


def coarse_block(vert, station):
    small = (8, 128)
    lane8, row8 = lanes_of(small), rows_of(small)
    group8 = lane8 // 32
    big = (16, 128)
    lane, row = lanes_of(big), rows_of(big)
    group = lane // 32
    low = [vert[every(half, 8, 4), :] for half in range(2)]
    high = [vert[every(2 + half, 8, 4), :] for half in range(2)]

    def turned(halves):
        parts = []
        for half in range(2):
            for turn in range(4):
                moved = roll(halves[half], 32 * turn)
                for bz in range(2):
                    mask = (group8 == row8 // 2) & (row8 % 2 == bz)
                    total = jnp.sum(jnp.where(mask, moved, 0.0), axis=0, keepdims=True)
                    parts.append((half, turn, bz, jnp.broadcast_to(total, big)))
        return parts

    def spread(parts, point, valid):
        out = jnp.zeros(big, F32)
        for half, turn, bz, total in parts:
            k = point - bz
            mask = (k >= 4 * half) & (k < 4 * half + 4) & (((group - k + 8) % 4) == turn) & valid
            out = out + jnp.where(mask, total, 0.0)
        return out

    main = turned([low[half] + from_below(high[half]) for half in range(2)])
    top = turned(high)
    block = spread(main, row, row < 9)
    last = lane % 32 == 31
    for third in range(3):
        moved = spread(top, row - 9 + 3 * third, (row >= 9) & (row < SENT))
        moved = jnp.where(last, moved, 0.0)
        block = block + pltpu.roll(moved, station // 2 + 8 * third + 97, 1)
    return block


def first_kernel(face_in, edge_in, vert_in, fturn_in, eturn_in, stiff_in,
                 xf_out, ef_out, xp_out, xm_out, zp_out, zm_out, cb_out, turns_out, weights_out,
                 xf, ef, xp, xm, zp, zm, cb, turns, weights,
                 face, edge, vert, fturn, sems, out_sems):
    copies = [
        pltpu.make_async_copy(source, target, sems.at[at])
        for at, (source, target) in enumerate((
            (vert_in, vert),
            (fturn_in, fturn),
            (eturn_in, turns.at[16:40]),
            (stiff_in, weights),
            (face_in.at[0:1448], face.at[0:1448]),
            (edge_in, edge),
            (face_in.at[1448:2904], face.at[1448:2904]),
        ))
    ]
    sent = []

    def send(source, target):
        copy = pltpu.make_async_copy(source, target, out_sems.at[len(sent)])
        copy.start()
        sent.append(copy)

    for copy in copies:
        copy.start()
    copies[0].wait()
    block = coarse_block(vert, lax.axis_index("gx"))
    for device in range(128):
        cb[device * SENT : device * SENT + SENT, :] = block[0:SENT]
    send(cb, cb_out)
    for copy in copies[1:]:
        copy.wait()
    for f in range(6):
        turns[2 * f : 2 * f + 2, :] = fturn[f]
    turns[12:16, :] = jnp.zeros((4, 128), jnp.int32)
    send(turns, turns_out)
    send(weights, weights_out)
    stiff = weights

    last = NODES - 1
    for half in range(2):
        turn = turns[every(half, 6, 2), :]
        swap, flip_a, flip_b = (turn & 4) != 0, (turn & 1) != 0, (turn & 2) != 0
        for s in range(2):
            source = s * 6 * 242 + half
            target = (half * 2 + s) * 6 * 128
            for group in ORBITS:
                x = {n: face[every(source + 2 * (n[0] * 11 + n[1]), 6, 242), :] for n in group}
                x = {(a, b): jnp.where(swap, x[b, a], x[a, b]) for a, b in group}
                x = {(a, b): jnp.where(flip_a, x[last - a, b], x[a, b]) for a, b in group}
                x = {(a, b): jnp.where(flip_b, x[a, last - b], x[a, b]) for a, b in group}
                for a, b in group:
                    xf[every(target + a * 11 + b, 6, 128), :] = x[a, b]
            for pad in range(121, 128):
                xf[every(target + pad, 6, 128), :] = jnp.zeros((6, 128), F32)
        mirror = turns[every(16 + half, 12, 2), :] != 0
        for s in range(2):
            source = s * 12 * 22 + half
            target = (half * 2 + s) * EDGE_ROWS
            x = [edge[every(source + 2 * p, 12, 22), :] for p in range(NODES)]
            for p in range(NODES):
                ef[every(target + p, 12, 16), :] = jnp.where(mirror, x[last - p], x[p])
            for pad in range(NODES, 16):
                ef[every(target + pad, 12, 16), :] = jnp.zeros((12, 128), F32)

    for half in range(2):
        weight = stiff[half : half + 1, :]
        for s in range(2):
            tile = half * 2 + s
            base = tile * SIDE_ROWS
            for ref, slot, edges in ((xp, 1, SENT_XP), (xm, 0, SENT_XM)):
                ref[base : base + 128, :] = xf[(tile * 6 + slot) * 128 : (tile * 6 + slot + 1) * 128, :]
                ref[base + 127 : base + 128, :] = weight
                for place, e in enumerate(edges):
                    ref[base + 128 + place * 16 : base + 144 + place * 16, :] = ef[
                        (tile * 12 + e) * 16 : (tile * 12 + e + 1) * 16, :
                    ]
    send(xp, xp_out)
    send(xm, xm_out)
    send(ef, ef_out)
    send(xf, xf_out)
    for ref, half, slot, edges in ((zp, 1, 3, SENT_ZP), (zm, 0, 2, SENT_ZM)):
        own = 96 if half else 0
        group = lanes_of((128, 128)) // 32
        faces = [
            roll(xf[((half * 2 + s) * 6 + slot) * 128 : ((half * 2 + s) * 6 + slot + 1) * 128, :],
                 32 * s - own)
            for s in range(2)
        ]
        lines = jnp.concatenate(
            [ef[((half * 2 + s) * 12 + e) * 16 : ((half * 2 + s) * 12 + e + 1) * 16, :]
             for s in range(2) for e in edges],
            axis=0,
        )
        weight = jnp.broadcast_to(roll(stiff[half : half + 1, :], 96 - own), (128, 128))
        out = jnp.where(group == 0, faces[0], faces[1])
        out = jnp.where(group == 2, roll(lines, 64 - own), out)
        ref[...] = jnp.where(group == 3, weight, out)
    send(zp, zp_out)
    send(zm, zm_out)
    for copy in sent:
        copy.wait()


def corner_kernel(zp, zm, rxm, rxp, out_p, out_m):
    lane, row = lanes_of((128, 128)), rows_of((128, 128))
    group = lane // 32
    for ref, out, half, place in ((zp, out_p, 1, 3), (zm, out_m, 0, 2)):
        own = 96 if half else 0
        out[...] = ref[...]
        for s in range(2):
            base = (half * 2 + s) * SIDE_ROWS + 128 + place * 16
            for third, side in ((2, rxm), (3, rxp)):
                at = s * 64 + third * 16
                moved = roll(side[base : base + 16, :], 64 - own)
                keep = lanes_of((16, 128)) // 32 == 2
                out[at : at + 16, :] += jnp.where(keep, moved, 0.0)
        for r, side in ((1, rxm), (2, rxp)):
            base = half * 2 * SIDE_ROWS + 127
            moved = roll(side[base : base + 1, :], 96 - own)
            out[r : r + 1, :] += jnp.where(lanes_of((1, 128)) >= 96, moved, 0.0)


def parameter_kernel(table_in, heights_in, diag_in, basis_in, eigs_in, ext_in,
                     table, lift, rdiag, heights, diag, basis, eigs, ext, work, sems):
    copies = [
        pltpu.make_async_copy(source, target, sems.at[at])
        for at, (source, target) in enumerate((
            (heights_in, heights), (diag_in, diag), (basis_in, basis), (eigs_in, eigs),
            (ext_in, ext), (table_in, table.at[0:PIVOTS]),
        ))
    ]
    for copy in copies:
        copy.start()
    for copy in copies:
        copy.wait()

    def dot(x, y):
        return jnp.dot(x, y, precision=HIGHEST, preferred_element_type=F32)

    def dot_first(x, y):
        return lax.dot_general(x, y, (((0,), (0,)), ((), ())), precision=HIGHEST,
                               preferred_element_type=F32)

    b = basis[...]
    cols_a, cols_b = table[PLACE["cols_a"], :], table[PLACE["cols_b"], :]
    modes = table[PLACE["modes"], :]
    kron = dot(dot_first(cols_a, b), cols_a) * dot(dot_first(cols_b, b), cols_b)
    scale = dot(eigs[...], cols_a + cols_b)
    scale = 1.0 / jnp.where(lanes_of((1, 128)) < FACE_NODES, scale, 1.0)
    work[...] = jnp.zeros((256, 128), F32)
    work[0:128, :] = lax.dot_general(
        kron * scale, kron, (((1,), (1,)), ((), ())), precision=HIGHEST,
        preferred_element_type=F32,
    )
    for place in range(4):
        work[128 + 16 * place : 139 + 16 * place, 0:FACE_NODES] = ext[11 * place : 11 * place + 11, :]
    work[192:196, 0:FACE_NODES] = ext[44:48, :]
    full = work[...].T
    high = full.astype(BF16)
    lift[0:128, :] = high
    lift[128:256, :] = (full - high.astype(F32)).astype(BF16)
    row = rows_of((16, 128))
    nodes = jnp.ones((16, 128), F32)
    for p in range(NODES):
        nodes = jnp.where(row == p, diag[0:1, p : p + 1], nodes)
    rdiag[...] = 1.0 / nodes

    wave = modes
    tall = [jnp.broadcast_to(heights[0:1, l : l + 1], (16, 128)) for l in range(LAYERS)]
    inverse = [1.0 / h for h in tall]
    prime = None
    for l in range(LEVELS):
        if l == 0:
            stiff, mass = inverse[0], 0.5 * tall[0]
        elif l == LAYERS:
            stiff, mass = inverse[l - 1], 0.5 * tall[l - 1]
        else:
            stiff, mass = inverse[l - 1] + inverse[l], 0.5 * (tall[l - 1] + tall[l])
        pivot = stiff + wave * mass
        if l:
            pivot = pivot - inverse[l - 1] * prime
        rp = 1.0 / pivot
        table[PIVOTS + l * 16 : PIVOTS + l * 16 + 16, :] = rp
        if l:
            table[CARRY + l * 16 : CARRY + l * 16 + 16, :] = inverse[l - 1] * rp
        else:
            table[CARRY : CARRY + 16, :] = jnp.zeros((16, 128), F32)
        if l < LAYERS:
            prime = inverse[l] * rp
            table[BACK + l * 16 : BACK + l * 16 + 16, :] = prime


def solve_kernel(g, table, v_out, v_hbm, vb_out, tz, px, zs, vs, ss, cs, sem):
    def dot(x, y):
        return jnp.dot(x, y, precision=HIGHEST, preferred_element_type=F32)

    stations = [g[x * STATION : x * STATION + STATION, :] for x in range(NX)]
    tz[...] = dot(table[PLACE["forward"], 0:STATION], jnp.concatenate(stations, axis=1))
    third = rows_of((128, 128)) % 32 // 8
    base_z, base_x = PLACE["top_z"].start, PLACE["top_x"].start
    tops = None
    for odd in range(2):
        total = stations[odd]
        for x in range(odd + 2, NX, 2):
            total = total + stations[x]
        total = jnp.concatenate([total, jnp.zeros((128 - STATION, 128), F32)], axis=0).T
        parts = [dot(total, table[base_z + 128 * q : base_z + 128 * q + 128, :]) for q in range(3)]
        part = jnp.where(third == 0, parts[0], jnp.where(third == 1, parts[1], parts[2]))
        part = dot(table[base_x + 32 * odd : base_x + 32 * odd + 32, :], part)
        tops = part if tops is None else tops + part
    mix = PLACE["mix"].start
    top = jnp.where(lanes_of((16, 128)) < 64, tops[0:16], tops[16:32])

    bx0 = lanes_of((16, 128)) // 32 % 2 == 0
    for m in range(4):
        t = [tz[m * 16 : m * 16 + 16, x * 128 : x * 128 + 128] for x in range(NX)]
        for kp in range(8):
            pair = []
            for par in range(2):
                k = kp * 2 + par
                acc = t[0] * table[mix + k * NX : mix + k * NX + 1, :]
                for x in range(1, NX):
                    acc = acc + t[x] * table[mix + k * NX + x : mix + k * NX + x + 1, :]
                pair.append(acc)
            even, odd = pair
            px[kp * 64 + m * 16 : kp * 64 + m * 16 + 16, :] = jnp.where(
                bx0, even + roll(even, 96), odd + roll(odd, 32)
            )
    for blk in range(4):
        turned = px[blk * 128 : blk * 128 + 128, :].T
        zs[blk * 64 : blk * 64 + 64, :] = turned[0:64]
        zs[256 + blk * 64 : 320 + blk * 64, :] = turned[64:128]

    value = None
    for l in range(LEVELS):
        rhs = zs[every(l, 16, 32), :] if l < LAYERS else top
        at = l * 16
        step = rhs * table[PIVOTS + at : PIVOTS + at + 16, :]
        value = step if l == 0 else step + table[CARRY + at : CARRY + at + 16, :] * value
        vs[at : at + 16, :] = value
    ss[...] = jnp.zeros((1024, 128), F32)
    for l in range(LEVELS - 1, -1, -1):
        if l < LEVELS - 1:
            at = l * 16
            value = vs[at : at + 16, :] + table[BACK + at : BACK + at + 16, :] * value
        ss[every(l, 16, 64), :] = value

    at = PLACE["back_z"].start + lax.axis_index("gz") * 32
    hz = table[pl.ds(pl.multiple_of(at, 16), 32), :]
    q = lax.dot_general(hz, ss[...], (((1,), (1,)), ((), ())), precision=HIGHEST,
                        preferred_element_type=F32)
    at = PLACE["back_x"].start + lax.axis_index("gx") * 16
    hx = table[pl.ds(pl.multiple_of(at, 16), 16), :]
    lane, row = lanes_of((16, 128)), rows_of((16, 128))
    group = lane // 32
    for s in range(2):
        for bx in range(2):
            acc = None
            for blk in range(4):
                for pair in range(2):
                    r = (bx * 4 + blk) * 2 + pair
                    term = q[pair * 16 : pair * 16 + 16, (s * 4 + blk) * 128 : (s * 4 + blk + 1) * 128]
                    term = term * hx[r : r + 1, :]
                    acc = term if acc is None else acc + term
            acc = acc + roll(acc, 64)
            for by in range(2):
                plain = roll(acc, 127) if by else acc
                moved = roll(plain, 32)
                mixed = jnp.where(group % 2 == 1, moved, plain)
                for bz in range(2):
                    base = (((s * 2 + bx) * 2 + by) * 2 + bz) * 16
                    keep = (row - bz + 4) % 4 == group
                    cs[base : base + 16, :] = jnp.where(keep, mixed, 0.0)
    picked = dot(table[PLACE["pick_0"], :], cs[0:128, :]) + dot(table[PLACE["pick_1"], :], cs[128:256, :])
    v_out[...] = picked[0:32]
    copy = pltpu.make_async_copy(v_out, v_hbm, sem)
    copy.start()
    vb_out[...] = picked[32:224]
    copy.wait()


def final_kernel(xf, ef, rxm, rxp, rzm, rzp, stiff, v, vb, lift, rdiag, turns,
                 face_hbm, edge_hbm, oq, ev, face_out, edge_out, sems):
    last = NODES - 1
    w = [stiff[half : half + 1, :] for half in range(2)]

    def tile(half, s, f):
        at = ((half * 2 + s) * 6 + f) * 128
        return xf[at : at + 128, :]

    def line(half, s, e):
        at = ((half * 2 + s) * 12 + e) * 16
        return ef[at : at + 16, :]

    def side_face(ref, half, s):
        at = (half * 2 + s) * SIDE_ROWS
        return ref[at : at + 128, :]

    def side_line(ref, half, s, place):
        at = (half * 2 + s) * SIDE_ROWS + 128 + place * 16
        return ref[at : at + 16, :]

    def side_weight(ref, half):
        at = half * 2 * SIDE_ROWS + 127
        return ref[at : at + 1, :]

    def halo_line(ref, s, place, to):
        at = s * 64 + place * 16
        return roll(ref[at : at + 16, :], to - 64)

    wxm = [w[half] + side_weight(rxm, half) for half in range(2)]
    wxp = [w[half] + side_weight(rxp, half) for half in range(2)]
    wzm_in = [roll(rzm[r : r + 1, :], 32) for r in range(3)]
    wzp_in = [rzp[r : r + 1, :] for r in range(3)]

    def add_before(pair, halo):
        moved = from_before(pair, halo)
        return [pair[0] + moved[0], pair[1] + moved[1]]

    def add_after(pair, halo):
        moved = from_after(pair, halo)
        return [pair[0] + moved[0], pair[1] + moved[1]]

    wzm, wzp = add_before(w, wzm_in[0]), add_after(w, wzp_in[0])
    corner = [add_before(wxm, wzm_in[1]), add_after(wxm, wzp_in[1]),
              add_before(wxp, wzm_in[2]), add_after(wxp, wzp_in[2])]
    below = lambda pair: [x + from_below(x) for x in pair]
    above = lambda pair: [x + from_above(x) for x in pair]
    covers = [below(wzm), above(wzm), below(wzp), above(wzp),
              below(wxm), above(wxm), below(wxp), above(wxp)] + corner
    face_covers = [wxm, wxp, wzm, wzp, below(w), above(w)]
    rec_face = [[1.0 / x for x in pair] for pair in face_covers]
    rec_edge = [[1.0 / x for x in pair] for pair in covers]

    row16 = rows_of((16, 128))
    high_t = (row16 + 1).astype(F32) / (NODES + 1.0)
    low_t = 1.0 - high_t
    diag = rdiag[...]
    copies = []

    for s in range(2):
        e = {}
        for half in range(2):
            for k in range(4):
                e[k, half] = line(half, s, k)
            for k, place in ((4, 0), (5, 1), (8, 2), (9, 3)):
                e[k, half] = line(half, s, k) + side_line(rxm, half, s, place)
            for k, place in ((6, 0), (7, 1), (10, 2), (11, 3)):
                e[k, half] = line(half, s, k) + side_line(rxp, half, s, place)
        both = lambda k: (e[k, 0], e[k, 1])
        sums = {}
        for k, other, place in ((0, 2, 0), (1, 3, 1), (8, 9, 2), (10, 11, 3)):
            moved = from_before(both(other), halo_line(rzm, s, place, 0))
            for half in range(2):
                sums[k, half] = e[k, half] + moved[half]
        for k, other, place in ((2, 0, 0), (3, 1, 1), (9, 8, 2), (11, 10, 3)):
            moved = from_after(both(other), halo_line(rzp, s, place, 96))
            for half in range(2):
                sums[k, half] = e[k, half] + moved[half]
        for k in range(4, 8):
            for half in range(2):
                sums[k, half] = e[k, half]
        for half in range(2):
            for k in range(0, 8, 2):
                a, b = sums[k, half], sums[k + 1, half]
                sums[k, half], sums[k + 1, half] = a + from_below(b), b + from_above(a)
            tilebase = (half * 2 + s) * EDGE_ROWS
            vertex = v[every(s * 16 + half, 8, 2), :]
            for k in range(12):
                start, stop = edge_ends(EDGE_SLOTS[k])
                local = sums[k, half] * (diag * rec_edge[k][half])
                ev[tilebase + k * 16 : tilebase + k * 16 + 16, :] = (
                    local + low_t * vertex[start : start + 1] + high_t * vertex[stop : stop + 1]
                )
        for half in range(2):
            columns = []
            for f in range(6):
                own = tile(half, s, f)
                if f == 0:
                    total = own + side_face(rxm, half, s)
                elif f == 1:
                    total = own + side_face(rxp, half, s)
                elif f == 2:
                    halo = roll(rzm[...], -32 * s)
                    total = own + from_before((tile(0, s, 3), tile(1, s, 3)), halo)[half]
                elif f == 3:
                    halo = roll(rzp[...], 96 - 32 * s)
                    total = own + from_after((tile(0, s, 2), tile(1, s, 2)), halo)[half]
                elif f == 4:
                    total = own + from_below(tile(half, s, 5))
                else:
                    total = own + from_above(tile(half, s, 4))
                edges = face_frame(FACE_SLOTS[f])[0]
                tilebase = (half * 2 + s) * EDGE_ROWS
                at = ((half * 2 + s) * 6 + f) * 8
                columns.append(jnp.concatenate(
                    [total * rec_face[f][half]]
                    + [ev[tilebase + k * 16 : tilebase + k * 16 + 16, :] for k in edges]
                    + [vb[at : at + 8, :], jnp.zeros((56, 128), F32)], axis=0))
            full = jnp.concatenate(columns, axis=1)
            high = full.astype(BF16)
            rest = (full - high.astype(F32)).astype(BF16)
            main = jnp.dot(lift[...], high, preferred_element_type=F32)
            more = jnp.dot(lift[0:128, :], rest, preferred_element_type=F32)
            done = main[0:128] + (main[128:256] + more)
            for f in range(6):
                at = ((half * 2 + s) * 6 + f) * 128
                oq[at : at + 128, :] = done[:, f * 128 : f * 128 + 128]

        for half in range(2):
            turn = turns[every(half, 6, 2), :]
            swap, flip_a, flip_b = (turn & 4) != 0, (turn & 1) != 0, (turn & 2) != 0
            target = s * 6 * 242 + half
            source = (half * 2 + s) * 6 * 128
            for group in ORBITS:
                x = {n: oq[every(source + n[0] * 11 + n[1], 6, 128), :] for n in group}
                x = {(a, b): jnp.where(flip_a, x[last - a, b], x[a, b]) for a, b in group}
                x = {(a, b): jnp.where(flip_b, x[a, last - b], x[a, b]) for a, b in group}
                x = {(a, b): jnp.where(swap, x[b, a], x[a, b]) for a, b in group}
                for a, b in group:
                    face_out[every(target + 2 * (a * 11 + b), 6, 242), :] = x[a, b]
            mirror = turns[every(16 + half, 12, 2), :] != 0
            target = s * 12 * 22 + half
            source = (half * 2 + s) * EDGE_ROWS
            x = [ev[every(source + p, 12, 16), :] for p in range(NODES)]
            for p in range(NODES):
                edge_out[every(target + 2 * p, 12, 22), :] = jnp.where(mirror, x[last - p], x[p])
        rows = (slice(0, 1448), slice(1448, 2904))[s]
        copies.append(pltpu.make_async_copy(face_out.at[rows], face_hbm.at[rows], sems.at[2 * s]))
        rows = slice(s * 264, s * 264 + 264)
        copies.append(pltpu.make_async_copy(edge_out.at[rows], edge_hbm.at[rows], sems.at[2 * s + 1]))
        for copy in copies[2 * s : 2 * s + 2]:
            copy.start()
    for copy in copies:
        copy.wait()


VMEM = pl.BlockSpec(memory_space=pltpu.VMEM)
HBM = pl.BlockSpec(memory_space=pltpu.HBM)


def call(kernel, name, args, ins, outs, out_specs, scratch=(), sems=(), flops=0,
         limit=VMEM_LIMIT):
    shapes = [jax.ShapeDtypeStruct(o, F32) if isinstance(o, tuple) else o for o in outs]
    held = [pltpu.VMEM(o, F32) if isinstance(o, tuple) else o for o in scratch]
    held += [pltpu.SemaphoreType.DMA(n) for n in sems]
    size = sum(int(np.prod(a.shape)) * 4 for a in args)
    return pl.pallas_call(
        kernel,
        out_shape=shapes,
        in_specs=ins,
        out_specs=out_specs,
        scratch_shapes=held,
        compiler_params=pltpu.CompilerParams(vmem_limit_bytes=limit),
        cost_estimate=pl.CostEstimate(flops=flops, bytes_accessed=size, transcendentals=0),
        name=name,
    )(*args)


def per_device(face_residual, edge_residual, vertex_residual, face_orient, edge_orient, stiffness,
               face_basis, face_eigs, extension, edge_diag, element_heights):
    face = face_residual.reshape(2904, 128)
    edge = edge_residual.reshape(528, 128)
    vert = vertex_residual.reshape(32, 128)
    fturn = face_orient.reshape(6, 2, 128)
    eturn = edge_orient.reshape(24, 128)
    stiff = stiffness.reshape(2, 128)
    tiles = 24 * 128
    kept = [(tiles, 128), (4 * EDGE_ROWS, 128), (4 * SIDE_ROWS, 128), (4 * SIDE_ROWS, 128),
            (128, 128), (128, 128), (128 * SENT, 128), (40, 128), (2, 128)]
    kinds = [F32] * 7 + [jnp.int32, F32]
    xf, ef, xp, xm, zp, zm, cb, turns, weights = call(
        first_kernel, "frame", (face, edge, vert, fturn, eturn, stiff), [HBM] * 6,
        [jax.ShapeDtypeStruct(o, kind) for o, kind in zip(kept, kinds)], [HBM] * 9,
        [pltpu.VMEM(o, kind) for o, kind in zip(kept, kinds)]
        + [(2904, 128), (528, 128), (32, 128), pltpu.VMEM((6, 2, 128), jnp.int32)],
        ((7,), (9,)), limit=VMEM_WHOLE)
    up = lambda n: [(i, (i + 1) % n) for i in range(n)]
    down = lambda n: [((i + 1) % n, i) for i in range(n)]
    rxm = lax.ppermute(xp, "gx", up(SPLIT_X))
    rxp = lax.ppermute(xm, "gx", down(SPLIT_X))
    table, lift, rdiag = call(
        parameter_kernel, "parameters",
        (jnp.asarray(TABLE), element_heights.reshape(1, LAYERS), edge_diag.reshape(1, NODES),
         face_basis, face_eigs.reshape(1, NODES), extension.T), [HBM] * 6,
        [(TABLE_ROWS, 128), jax.ShapeDtypeStruct((256, 256), BF16), (16, 128)], [VMEM] * 3,
        ((1, LAYERS), (1, NODES), (NODES, NODES), (1, NODES), (48, FACE_NODES), (256, 128)), ((6,),))
    g = lax.all_to_all(cb.reshape(128, 3, 4, 128), ("gx", "gz"), 0, 0)
    g = g.reshape(128 * SENT, 128)
    zp, zm = call(corner_kernel, "corners", (zp, zm, rxm, rxp), [VMEM] * 4,
                  [(128, 128), (128, 128)], [VMEM] * 2, flops=CORNER_FLOPS)
    rzm = lax.ppermute(zp, "gz", up(SPLIT_Z))
    rzp = lax.ppermute(zm, "gz", down(SPLIT_Z))
    v, v_out, vb = call(
        solve_kernel, "coarse", (g, table), [VMEM] * 2, [(32, 128), (32, 128), (192, 128)],
        [VMEM, HBM, VMEM],
        ((64, 2048), (512, 128), (512, 128), (LEVELS * 16, 128), (1024, 128), (256, 128)), ((),),
        flops=200_000_000)
    face_out, edge_out = call(
        final_kernel, "finish",
        (xf, ef, rxm, rxp, rzm, rzp, weights, v, vb, lift, rdiag, turns), [VMEM] * 12,
        [(2904, 128), (528, 128)], [HBM] * 2,
        ((tiles, 128), (4 * EDGE_ROWS, 128), (2904, 128), (528, 128)), ((4,),))
    return (face_out.reshape(face_residual.shape), edge_out.reshape(edge_residual.shape),
            v_out.reshape(vertex_residual.shape))


def solution(mesh):
    columns = P(None, None, None, "gx", "gz")
    placed = (columns, columns, P(None, None, "gx", "gz"), P(None, "gx", "gz"),
              P(None, "gx", "gz"), P("gx", "gz"), P(), P(), P(), P(), P())
    return jax.shard_map(
        per_device, mesh=mesh, in_specs=placed,
        out_specs=(columns, columns, P(None, None, "gx", "gz")), check_vma=False)
```

```python
import math

import jax
import jax.numpy as jnp
import numpy as np
from jax import lax
from jax.experimental import pallas as pl
from jax.experimental.pallas import tpu as pltpu
from jax.sharding import PartitionSpec as P

F32 = jnp.float32
BF16 = jnp.bfloat16
HIGHEST = lax.Precision.HIGHEST
SHIFT_MASS = 0.004
NX, NZ, LAYERS, LEVELS, NODES = 16, 64, 32, 33, 11
SPLIT_X, SPLIT_Z, OWN_Z = 16, 8, 8
FACE_NODES = 121
EDGE_ROWS = 16 * 12
SIDE_ROWS = 192
SENT = 12
STATION = SENT * SPLIT_Z
VMEM_LIMIT = 24 * 1024 * 1024
CORNER_FLOPS = 100_000_000_000
VMEM_WHOLE = 60 * 1024 * 1024

FACE_SLOTS = ((-1, 0, 0), (1, 0, 0), (0, -1, 0), (0, 1, 0), (0, 0, -1), (0, 0, 1))
EDGE_SLOTS = (
    (0, -1, -1), (0, -1, 1), (0, 1, -1), (0, 1, 1),
    (-1, 0, -1), (-1, 0, 1), (1, 0, -1), (1, 0, 1),
    (-1, -1, 0), (-1, 1, 0), (1, -1, 0), (1, 1, 0),
)
VERTEX_SLOTS = tuple((x, z, y) for x in (-1, 1) for z in (-1, 1) for y in (-1, 1))
SENT_XP, SENT_XM = (6, 7, 10, 11), (4, 5, 8, 9)
SENT_ZP, SENT_ZM = (2, 3, 9, 11), (0, 1, 8, 10)


def orbits():
    seen, result = set(), []
    last = NODES - 1
    for a in range(NODES):
        for b in range(NODES):
            if (a, b) in seen:
                continue
            group, queue = [], [(a, b)]
            while queue:
                node = queue.pop()
                if node in seen:
                    continue
                seen.add(node)
                group.append(node)
                p, q = node
                queue += [(q, p), (last - p, q), (p, last - q)]
            result.append(group)
    return result


ORBITS = orbits()


def face_frame(slot):
    tangents = [axis for axis in range(3) if slot[axis] == 0]
    edges, corners = [], []
    for axis in tangents:
        for sign in (-1, 1):
            corner = list(slot)
            corner[axis] = sign
            edges.append(EDGE_SLOTS.index(tuple(corner)))
    for first in (-1, 1):
        for second in (-1, 1):
            corner = list(slot)
            corner[tangents[0]] = first
            corner[tangents[1]] = second
            corners.append(VERTEX_SLOTS.index(tuple(corner)))
    return edges, corners


def edge_ends(slot):
    axis = slot.index(0)
    ends = []
    for sign in (-1, 1):
        point = list(slot)
        point[axis] = sign
        ends.append(VERTEX_SLOTS.index(tuple(point)))
    return ends


def hartley_table(size):
    phase = np.outer(np.arange(size), np.arange(size)) % size
    angle = 2.0 * np.pi / size * phase
    return (np.cos(angle) + np.sin(angle)) / math.sqrt(size)


HX, HZ = hartley_table(NX), hartley_table(NZ)


def build_tables():
    f32 = lambda a: np.ascontiguousarray(a, dtype=np.float32)
    tables = {}
    forward = np.zeros((128, 2 * NZ))
    top_z = np.zeros((3, 128, 2 * NZ))
    for gz in range(SPLIT_Z):
        for kk in range(9):
            column = HZ[:, (8 * gz + kk) % NZ]
            forward[gz * SENT + kk] = np.tile(column, 2)
            top_z[kk // 3, gz * SENT + 9 + kk % 3] = np.tile(column, 2)
    tables["forward"] = f32(forward)
    tables["top_z"] = f32(top_z.reshape(3 * 128, 128))
    lane = np.arange(128)
    lane_s, lane_bx, lane_j = lane // 64, lane // 32 % 2, lane % 32
    mix = np.zeros((NX // 2, NX, 2, NZ))
    for k in range(NX):
        for x in range(NX):
            mix[k // 2, x, k % 2] = HX[k, x]
    tables["mix"] = f32(mix.reshape(NX * NX // 2, 128))
    top_x = np.zeros((2, 2, 16, 128))
    modes = np.zeros((16, 128))
    waves_x = 2.0 - 2.0 * np.cos(2.0 * np.pi / NX * np.arange(NX))
    waves_z = 2.0 - 2.0 * np.cos(2.0 * np.pi / NZ * np.arange(NZ))
    for row in range(16):
        s = row // 8
        for pair in range(2):
            k = row % 8 * 2 + pair
            for odd in range(2):
                x = 2 * (lane_j % 8) + odd
                top_x[odd, pair, row] = np.where(lane_s == s, HX[k, (x + lane_bx) % NX], 0.0)
            modes[row, pair * 64 : pair * 64 + 64] = waves_x[k] + waves_z + SHIFT_MASS
    tables["top_x"] = f32(top_x.reshape(64, 128))
    tables["modes"] = f32(modes)
    back_z = np.zeros((SPLIT_Z, 16, 2 * NZ))
    for gz in range(SPLIT_Z):
        for kk in range(9):
            back_z[gz, kk] = np.tile(HZ[(8 * gz + kk) % NZ], 2)
    tables["back_z"] = f32(back_z.reshape(SPLIT_Z * 16, 128))
    back_x = np.zeros((SPLIT_X, 2, 8, 2, NZ))
    for gx in range(SPLIT_X):
        for bx in range(2):
            for k in range(NX):
                back_x[gx, bx, k // 2, k % 2] = HX[(gx + bx) % NX, k]
    tables["back_x"] = f32(back_x.reshape(SPLIT_X * 16, 128))
    pick = np.zeros((32 + 192, 256))

    def fill(row, s, corner, half):
        bx, bz, by = corner // 4, corner // 2 % 2, corner % 2
        base = (((s * 2 + bx) * 2 + by) * 2 + bz) * 16
        for k in range(4):
            pick[row, base + half * 4 + k + bz] = 1.0

    for s in range(2):
        for half in range(2):
            for corner in range(8):
                fill((s * 8 + corner) * 2 + half, s, corner, half)
            for face, slot in enumerate(FACE_SLOTS):
                for place, corner in enumerate(face_frame(slot)[1]):
                    fill(32 + ((half * 2 + s) * 6 + face) * 8 + place, s, corner, half)
    tables["pick"] = f32(pick)
    expand = np.zeros((2, 128, NODES))
    for q in range(FACE_NODES):
        expand[0, q, q // NODES] = 1.0
        expand[1, q, q % NODES] = 1.0
    tables["cols_a"], tables["cols_b"] = f32(expand[0].T), f32(expand[1].T)
    for name in ("pick",):
        wide = tables.pop(name)
        tables[name + "_0"], tables[name + "_1"] = f32(wide[:, :128]), f32(wide[:, 128:])
    rows, places, pieces = 0, {}, []
    for name, value in tables.items():
        count = -(-value.shape[0] // 16) * 16
        places[name] = slice(rows, rows + value.shape[0])
        pieces.append(np.pad(value, ((0, count - value.shape[0]), (0, 0))))
        rows += count
    return f32(np.concatenate(pieces, axis=0)), places


TABLE, PLACE = build_tables()
PIVOTS = TABLE.shape[0]
CARRY = PIVOTS + LEVELS * 16
BACK = CARRY + LEVELS * 16
TABLE_ROWS = BACK + LAYERS * 16


def lanes_of(shape):
    return lax.broadcasted_iota(jnp.int32, shape, 1)


def rows_of(shape):
    return lax.broadcasted_iota(jnp.int32, shape, 0)


def roll(value, shift):
    return pltpu.roll(value, shift % 128, 1)


def every(start, size, stride):
    return pl.ds(start, size, stride=stride)


def from_below(low, high=None):
    lane = lanes_of(low.shape)
    return jnp.where(lane % 32 > 0, roll(low, 1), 0.0)


def from_above(value):
    lane = lanes_of(value.shape)
    return jnp.where(lane % 32 < 31, roll(value, -1), 0.0)


def from_before(pair, halo):
    first, second = roll(pair[0], 32), roll(pair[1], 32)
    head = lanes_of(first.shape) < 32
    return jnp.where(head, halo, first), jnp.where(head, first, second)


def from_after(pair, halo):
    first, second = roll(pair[0], 96), roll(pair[1], 96)
    tail = lanes_of(first.shape) >= 96
    return jnp.where(tail, second, first), jnp.where(tail, halo, second)


def coarse_block(vert, station):
    small = (8, 128)
    lane8, row8 = lanes_of(small), rows_of(small)
    group8 = lane8 // 32
    big = (16, 128)
    lane, row = lanes_of(big), rows_of(big)
    group = lane // 32
    low = [vert[every(half, 8, 4), :] for half in range(2)]
    high = [vert[every(2 + half, 8, 4), :] for half in range(2)]

    def turned(halves):
        parts = []
        for half in range(2):
            for turn in range(4):
                moved = roll(halves[half], 32 * turn)
                for bz in range(2):
                    mask = (group8 == row8 // 2) & (row8 % 2 == bz)
                    total = jnp.sum(jnp.where(mask, moved, 0.0), axis=0, keepdims=True)
                    parts.append((half, turn, bz, jnp.broadcast_to(total, big)))
        return parts

    def spread(parts, point, valid):
        out = jnp.zeros(big, F32)
        for half, turn, bz, total in parts:
            k = point - bz
            mask = (k >= 4 * half) & (k < 4 * half + 4) & (((group - k + 8) % 4) == turn) & valid
            out = out + jnp.where(mask, total, 0.0)
        return out

    main = turned([low[half] + from_below(high[half]) for half in range(2)])
    top = turned(high)
    block = spread(main, row, row < 9)
    last = lane % 32 == 31
    for third in range(3):
        moved = spread(top, row - 9 + 3 * third, (row >= 9) & (row < SENT))
        moved = jnp.where(last, moved, 0.0)
        block = block + pltpu.roll(moved, station // 2 + 8 * third + 97, 1)
    return block


def first_kernel(face_in, edge_in, vert_in, fturn_in, eturn_in, stiff_in,
                 xf_out, ef_out, near_out, far_out, zp_out, zm_out, cb_out, turns_out, weights_out,
                 xf, ef, near, far, zp, zm, cb, turns, weights,
                 face, edge, vert, fturn, sems, out_sems):
    copies = [
        pltpu.make_async_copy(source, target, sems.at[at])
        for at, (source, target) in enumerate((
            (vert_in, vert),
            (fturn_in, fturn),
            (eturn_in, turns.at[16:40]),
            (stiff_in, weights),
            (face_in.at[0:1456], face.at[0:1456]),
            (edge_in, edge),
            (face_in.at[1456:2904], face.at[1456:2904]),
        ))
    ]
    sent = []

    def send(source, target):
        copy = pltpu.make_async_copy(source, target, out_sems.at[len(sent)])
        copy.start()
        sent.append(copy)

    for copy in copies:
        copy.start()
    copies[0].wait()
    block = coarse_block(vert, lax.axis_index("gx"))
    for device in range(128):
        cb[device * SENT : device * SENT + SENT, :] = block[0:SENT]
    send(cb, cb_out)
    for at in (1, 2, 3, 5):
        copies[at].wait()
    for f in range(6):
        turns[2 * f : 2 * f + 2, :] = fturn[f]
    turns[12:16, :] = jnp.zeros((4, 128), jnp.int32)
    send(turns, turns_out)
    send(weights, weights_out)
    stiff = weights

    last = NODES - 1
    first_core = lax.axis_index("gx") % 2 == 0
    mirrors, masks = [], []
    for half in range(2):
        turn = turns[every(half, 6, 2), :]
        masks.append(((turn & 4) != 0, (turn & 1) != 0, (turn & 2) != 0))
        mirrors.append(turns[every(16 + half, 12, 2), :] != 0)
    for half in range(2):
        for s in range(2):
            if half == 0:
                copies[4 + 2 * s].wait()
            swap, flip_a, flip_b = masks[half]
            source = s * 6 * 242 + half
            tile = half * 2 + s
            target = tile * 6 * 128
            for group in ORBITS:
                x = {n: face[every(source + 2 * (n[0] * 11 + n[1]), 6, 242), :] for n in group}
                x = {(a, b): jnp.where(swap, x[b, a], x[a, b]) for a, b in group}
                x = {(a, b): jnp.where(flip_a, x[last - a, b], x[a, b]) for a, b in group}
                x = {(a, b): jnp.where(flip_b, x[a, last - b], x[a, b]) for a, b in group}
                for a, b in group:
                    xf[every(target + a * 11 + b, 6, 128), :] = x[a, b]
            for pad in range(121, 128):
                xf[every(target + pad, 6, 128), :] = jnp.zeros((6, 128), F32)
            send(xf.at[target : target + 768], xf_out.at[target : target + 768])
            source = s * 12 * 22 + half
            target = tile * EDGE_ROWS
            x = [edge[every(source + 2 * p, 12, 22), :] for p in range(NODES)]
            for p in range(NODES):
                ef[every(target + p, 12, 16), :] = jnp.where(mirrors[half], x[last - p], x[p])
            for pad in range(NODES, 16):
                ef[every(target + pad, 12, 16), :] = jnp.zeros((12, 128), F32)
            send(ef.at[target : target + EDGE_ROWS], ef_out.at[target : target + EDGE_ROWS])
            base = tile * SIDE_ROWS
            up = xf[(tile * 6 + 1) * 128 : (tile * 6 + 2) * 128, :]
            down = xf[tile * 6 * 128 : (tile * 6 + 1) * 128, :]
            near[base : base + 128, :] = jnp.where(first_core, up, down)
            far[base : base + 128, :] = jnp.where(first_core, down, up)
            for ref in (near, far):
                ref[base + 127 : base + 128, :] = stiff[half : half + 1, :]
            for place in range(4):
                up_at = (tile * 12 + SENT_XP[place]) * 16
                down_at = (tile * 12 + SENT_XM[place]) * 16
                up, down = ef[up_at : up_at + 16, :], ef[down_at : down_at + 16, :]
                at = base + 128 + place * 16
                near[at : at + 16, :] = jnp.where(first_core, up, down)
                far[at : at + 16, :] = jnp.where(first_core, down, up)
            for ref, out in ((near, near_out), (far, far_out)):
                send(ref.at[base : base + SIDE_ROWS], out.at[base : base + SIDE_ROWS])

    for ref, half, slot, edges in ((zp, 1, 3, SENT_ZP), (zm, 0, 2, SENT_ZM)):
        own = 96 if half else 0
        group = lanes_of((128, 128)) // 32
        faces = [
            roll(xf[((half * 2 + s) * 6 + slot) * 128 : ((half * 2 + s) * 6 + slot + 1) * 128, :],
                 32 * s - own)
            for s in range(2)
        ]
        lines = jnp.concatenate(
            [ef[((half * 2 + s) * 12 + e) * 16 : ((half * 2 + s) * 12 + e + 1) * 16, :]
             for s in range(2) for e in edges],
            axis=0,
        )
        weight = jnp.broadcast_to(roll(stiff[half : half + 1, :], 96 - own), (128, 128))
        out = jnp.where(group == 0, faces[0], faces[1])
        out = jnp.where(group == 2, roll(lines, 64 - own), out)
        ref[...] = jnp.where(group == 3, weight, out)
    send(zp, zp_out)
    send(zm, zm_out)
    for copy in sent:
        copy.wait()


class Side:
    def __init__(self, first, second):
        self.first, self.second = first, second
        self.core = lax.axis_index("gx") % 2 == 0

    def __getitem__(self, at):
        return jnp.where(self.core, self.first[at], self.second[at])


def corner_kernel(zp, zm, near, far, out_p, out_m):
    rxm, rxp = Side(far, near), Side(near, far)
    lane, row = lanes_of((128, 128)), rows_of((128, 128))
    group = lane // 32
    for ref, out, half, place in ((zp, out_p, 1, 3), (zm, out_m, 0, 2)):
        own = 96 if half else 0
        out[...] = ref[...]
        for s in range(2):
            base = (half * 2 + s) * SIDE_ROWS + 128 + place * 16
            for third, side in ((2, rxm), (3, rxp)):
                at = s * 64 + third * 16
                moved = roll(side[base : base + 16, :], 64 - own)
                keep = lanes_of((16, 128)) // 32 == 2
                out[at : at + 16, :] += jnp.where(keep, moved, 0.0)
        for r, side in ((1, rxm), (2, rxp)):
            base = half * 2 * SIDE_ROWS + 127
            moved = roll(side[base : base + 1, :], 96 - own)
            out[r : r + 1, :] += jnp.where(lanes_of((1, 128)) >= 96, moved, 0.0)


def parameter_kernel(table_in, heights_in, diag_in, basis_in, eigs_in, ext_in,
                     table, lift, rdiag, heights, diag, basis, eigs, ext, work, sems):
    copies = [
        pltpu.make_async_copy(source, target, sems.at[at])
        for at, (source, target) in enumerate((
            (heights_in, heights), (diag_in, diag), (basis_in, basis), (eigs_in, eigs),
            (ext_in, ext), (table_in, table.at[0:PIVOTS]),
        ))
    ]
    for copy in copies:
        copy.start()
    for copy in copies:
        copy.wait()

    def dot(x, y):
        return jnp.dot(x, y, precision=HIGHEST, preferred_element_type=F32)

    def dot_first(x, y):
        return lax.dot_general(x, y, (((0,), (0,)), ((), ())), precision=HIGHEST,
                               preferred_element_type=F32)

    b = basis[...]
    cols_a, cols_b = table[PLACE["cols_a"], :], table[PLACE["cols_b"], :]
    modes = table[PLACE["modes"], :]
    kron = dot(dot_first(cols_a, b), cols_a) * dot(dot_first(cols_b, b), cols_b)
    scale = dot(eigs[...], cols_a + cols_b)
    scale = 1.0 / jnp.where(lanes_of((1, 128)) < FACE_NODES, scale, 1.0)
    work[...] = jnp.zeros((256, 128), F32)
    work[0:128, :] = lax.dot_general(
        kron * scale, kron, (((1,), (1,)), ((), ())), precision=HIGHEST,
        preferred_element_type=F32,
    )
    for place in range(4):
        work[128 + 16 * place : 139 + 16 * place, 0:FACE_NODES] = ext[11 * place : 11 * place + 11, :]
    work[192:196, 0:FACE_NODES] = ext[44:48, :]
    full = work[...].T
    high = full.astype(BF16)
    lift[0:128, :] = high
    lift[128:256, :] = (full - high.astype(F32)).astype(BF16)
    row = rows_of((16, 128))
    nodes = jnp.ones((16, 128), F32)
    for p in range(NODES):
        nodes = jnp.where(row == p, diag[0:1, p : p + 1], nodes)
    rdiag[...] = 1.0 / nodes

    tall = [jnp.broadcast_to(heights[0:1, l : l + 1], (16, 128)) for l in range(LAYERS)]
    inverse = [1.0 / h for h in tall]
    prime = None
    for l in range(LEVELS):
        if l == 0:
            stiff, mass = inverse[0], 0.5 * tall[0]
        elif l == LAYERS:
            stiff, mass = inverse[l - 1], 0.5 * tall[l - 1]
        else:
            stiff, mass = inverse[l - 1] + inverse[l], 0.5 * (tall[l - 1] + tall[l])
        pivot = stiff + modes * mass
        if l:
            pivot = pivot - inverse[l - 1] * prime
        rp = 1.0 / pivot
        table[PIVOTS + l * 16 : PIVOTS + l * 16 + 16, :] = rp
        if l:
            table[CARRY + l * 16 : CARRY + l * 16 + 16, :] = inverse[l - 1] * rp
        else:
            table[CARRY : CARRY + 16, :] = jnp.zeros((16, 128), F32)
        if l < LAYERS:
            prime = inverse[l] * rp
            table[BACK + l * 16 : BACK + l * 16 + 16, :] = prime


def thirds(value):
    high = value.astype(BF16)
    rest = value - high.astype(F32)
    middle = rest.astype(BF16)
    return high, middle, (rest - middle.astype(F32)).astype(BF16)


def solve_kernel(g, table, v_out, v_hbm, vb_out, tz, zs, vs, ss, cs, sem):
    def dot(x, y):
        return jnp.dot(x, y, precision=HIGHEST, preferred_element_type=F32)

    pad = jnp.zeros((128 - STATION, 128), F32)
    stations = []
    for x in range(NX):
        station = g[x * STATION : x * STATION + STATION, :]
        stations.append(jnp.concatenate([station, pad], axis=0).T)
    high, middle, low = thirds(jnp.concatenate(stations, axis=0))
    wave = thirds(table[PLACE["forward"], :])
    both = jnp.concatenate(wave[0:2], axis=1)
    main = jnp.dot(jnp.concatenate([high, middle], axis=1), jnp.concatenate([both, both], axis=0),
                   preferred_element_type=F32)
    more = jnp.dot(jnp.concatenate([high, low], axis=1),
                   jnp.concatenate([wave[2], wave[0]], axis=0), preferred_element_type=F32)
    tz[...] = main[:, 0:128] + (main[:, 128:256] + more)
    third = rows_of((128, 128)) % 32 // 8
    base_z, base_x = PLACE["top_z"].start, PLACE["top_x"].start
    tops = None
    for odd in range(2):
        total = stations[odd]
        for x in range(odd + 2, NX, 2):
            total = total + stations[x]
        parts = [dot(total, table[base_z + 128 * q : base_z + 128 * q + 128, :]) for q in range(3)]
        part = jnp.where(third == 0, parts[0], jnp.where(third == 1, parts[1], parts[2]))
        part = dot(table[base_x + 32 * odd : base_x + 32 * odd + 32, :], part)
        tops = part if tops is None else tops + part
    mix = PLACE["mix"].start
    top = jnp.where(lanes_of((16, 128)) < 64, tops[0:16], tops[16:32])

    for s in range(2):
        for j in (0, 16):
            at = s * 64 + j
            parts = []
            for x in range(NX):
                near, far = x * 128 + at, (x + NX - 1) % NX * 128 + at + 32
                parts.append(tz[near : near + 16, :] + tz[far : far + 16, :])
            for pair in range(NX // 2):
                row = mix + pair * NX
                acc = parts[0] * table[row : row + 1, :]
                for x in range(1, NX):
                    acc = acc + parts[x] * table[row + x : row + x + 1, :]
                to = (s * 8 + pair) * 32 + j
                zs[to : to + 16, :] = acc

    value = None
    for l in range(LEVELS):
        rhs = zs[every(l, 16, 32), :] if l < LAYERS else top
        at = l * 16
        step = rhs * table[PIVOTS + at : PIVOTS + at + 16, :]
        value = step if l == 0 else step + table[CARRY + at : CARRY + at + 16, :] * value
        vs[at : at + 16, :] = value
    for l in range(LEVELS - 1, -1, -1):
        if l < LEVELS - 1:
            at = l * 16
            value = vs[at : at + 16, :] + table[BACK + at : BACK + at + 16, :] * value
        ss[every(l, 16, 64), :] = value
    for l in range(LEVELS, 40):
        ss[every(l, 16, 64), :] = jnp.zeros((16, 128), F32)

    at = PLACE["back_x"].start + lax.axis_index("gx") * 16
    hx = table[pl.ds(pl.multiple_of(at, 16), 16), :]
    columns = []
    for s in range(2):
        for bx in range(2):
            acc = None
            for t in range(8):
                r = bx * 8 + t
                term = ss[(s * 8 + t) * 64 : (s * 8 + t) * 64 + 40, :] * hx[r : r + 1, :]
                acc = term if acc is None else acc + term
            columns += [acc, jnp.zeros((24, 128), F32)]
    at = PLACE["back_z"].start + lax.axis_index("gz") * 16
    hz = table[pl.ds(pl.multiple_of(at, 16), 16), :]
    q = lax.dot_general(hz, jnp.concatenate(columns, axis=0), (((1,), (1,)), ((), ())),
                        precision=HIGHEST, preferred_element_type=F32)
    lane, row = lanes_of((16, 128)), rows_of((16, 128))
    group = lane // 32
    for s in range(2):
        near = q[:, s * 128 : s * 128 + 128]
        far = roll(near, 64)
        for bx in range(2):
            acc = jnp.where((lane < 64) == (bx == 0), near, far)
            for by in range(2):
                plain = roll(acc, 127) if by else acc
                moved = roll(plain, 32)
                mixed = jnp.where(group % 2 == 1, moved, plain)
                for bz in range(2):
                    base = (((s * 2 + bx) * 2 + by) * 2 + bz) * 16
                    keep = (row - bz + 4) % 4 == group
                    cs[base : base + 16, :] = jnp.where(keep, mixed, 0.0)
    pick = jnp.concatenate(
        [table[PLACE["pick_0"], :].astype(BF16), table[PLACE["pick_1"], :].astype(BF16)], axis=1)
    rest, picked = cs[...], None
    for _ in range(3):
        part = rest.astype(BF16)
        rest = rest - part.astype(F32)
        chosen = jnp.dot(pick, part, preferred_element_type=F32)
        picked = chosen if picked is None else picked + chosen
    v_out[...] = picked[0:32]
    copy = pltpu.make_async_copy(v_out, v_hbm, sem)
    copy.start()
    vb_out[...] = picked[32:224]
    copy.wait()


def final_kernel(xf, ef, near, far, rzm, rzp, stiff, v, vb, lift, rdiag, turns,
                 face_hbm, edge_hbm, oq, ev, face_out, edge_out, sems):
    last = NODES - 1
    rxm, rxp = Side(far, near), Side(near, far)
    w = [stiff[half : half + 1, :] for half in range(2)]

    def tile(half, s, f):
        at = ((half * 2 + s) * 6 + f) * 128
        return xf[at : at + 128, :]

    def line(half, s, e):
        at = ((half * 2 + s) * 12 + e) * 16
        return ef[at : at + 16, :]

    def side_face(ref, half, s):
        at = (half * 2 + s) * SIDE_ROWS
        return ref[at : at + 128, :]

    def side_line(ref, half, s, place):
        at = (half * 2 + s) * SIDE_ROWS + 128 + place * 16
        return ref[at : at + 16, :]

    def side_weight(ref, half):
        at = half * 2 * SIDE_ROWS + 127
        return ref[at : at + 1, :]

    def halo_line(ref, s, place, to):
        at = s * 64 + place * 16
        return roll(ref[at : at + 16, :], to - 64)

    wxm = [w[half] + side_weight(rxm, half) for half in range(2)]
    wxp = [w[half] + side_weight(rxp, half) for half in range(2)]
    wzm_in = [roll(rzm[r : r + 1, :], 32) for r in range(3)]
    wzp_in = [rzp[r : r + 1, :] for r in range(3)]

    def add_before(pair, halo):
        moved = from_before(pair, halo)
        return [pair[0] + moved[0], pair[1] + moved[1]]

    def add_after(pair, halo):
        moved = from_after(pair, halo)
        return [pair[0] + moved[0], pair[1] + moved[1]]

    wzm, wzp = add_before(w, wzm_in[0]), add_after(w, wzp_in[0])
    corner = [add_before(wxm, wzm_in[1]), add_after(wxm, wzp_in[1]),
              add_before(wxp, wzm_in[2]), add_after(wxp, wzp_in[2])]
    below = lambda pair: [x + from_below(x) for x in pair]
    above = lambda pair: [x + from_above(x) for x in pair]
    covers = [below(wzm), above(wzm), below(wzp), above(wzp),
              below(wxm), above(wxm), below(wxp), above(wxp)] + corner
    face_covers = [wxm, wxp, wzm, wzp, below(w), above(w)]
    rec_face = [[1.0 / x for x in pair] for pair in face_covers]
    rec_edge = [[1.0 / x for x in pair] for pair in covers]

    row16 = rows_of((16, 128))
    high_t = (row16 + 1).astype(F32) / (NODES + 1.0)
    low_t = 1.0 - high_t
    diag = rdiag[...]
    copies = []

    for s in range(2):
        e = {}
        for half in range(2):
            for k in range(4):
                e[k, half] = line(half, s, k)
            for k, place in ((4, 0), (5, 1), (8, 2), (9, 3)):
                e[k, half] = line(half, s, k) + side_line(rxm, half, s, place)
            for k, place in ((6, 0), (7, 1), (10, 2), (11, 3)):
                e[k, half] = line(half, s, k) + side_line(rxp, half, s, place)
        both = lambda k: (e[k, 0], e[k, 1])
        sums = {}
        for k, other, place in ((0, 2, 0), (1, 3, 1), (8, 9, 2), (10, 11, 3)):
            moved = from_before(both(other), halo_line(rzm, s, place, 0))
            for half in range(2):
                sums[k, half] = e[k, half] + moved[half]
        for k, other, place in ((2, 0, 0), (3, 1, 1), (9, 8, 2), (11, 10, 3)):
            moved = from_after(both(other), halo_line(rzp, s, place, 96))
            for half in range(2):
                sums[k, half] = e[k, half] + moved[half]
        for k in range(4, 8):
            for half in range(2):
                sums[k, half] = e[k, half]
        for half in range(2):
            for k in range(0, 8, 2):
                a, b = sums[k, half], sums[k + 1, half]
                sums[k, half], sums[k + 1, half] = a + from_below(b), b + from_above(a)
            tilebase = (half * 2 + s) * EDGE_ROWS
            vertex = v[every(s * 16 + half, 8, 2), :]
            for k in range(12):
                start, stop = edge_ends(EDGE_SLOTS[k])
                local = sums[k, half] * (diag * rec_edge[k][half])
                ev[tilebase + k * 16 : tilebase + k * 16 + 16, :] = (
                    local + low_t * vertex[start : start + 1] + high_t * vertex[stop : stop + 1]
                )
        for half in range(2):
            columns = []
            for f in range(6):
                own = tile(half, s, f)
                if f == 0:
                    total = own + side_face(rxm, half, s)
                elif f == 1:
                    total = own + side_face(rxp, half, s)
                elif f == 2:
                    halo = roll(rzm[...], -32 * s)
                    total = own + from_before((tile(0, s, 3), tile(1, s, 3)), halo)[half]
                elif f == 3:
                    halo = roll(rzp[...], 96 - 32 * s)
                    total = own + from_after((tile(0, s, 2), tile(1, s, 2)), halo)[half]
                elif f == 4:
                    total = own + from_below(tile(half, s, 5))
                else:
                    total = own + from_above(tile(half, s, 4))
                edges = face_frame(FACE_SLOTS[f])[0]
                tilebase = (half * 2 + s) * EDGE_ROWS
                at = ((half * 2 + s) * 6 + f) * 8
                columns.append(jnp.concatenate(
                    [total * rec_face[f][half]]
                    + [ev[tilebase + k * 16 : tilebase + k * 16 + 16, :] for k in edges]
                    + [vb[at : at + 8, :], jnp.zeros((56, 128), F32)], axis=0))
            full = jnp.concatenate(columns, axis=1)
            high = full.astype(BF16)
            rest = (full - high.astype(F32)).astype(BF16)
            main = jnp.dot(lift[...], high, preferred_element_type=F32)
            more = jnp.dot(lift[0:128, :], rest, preferred_element_type=F32)
            done = main[0:128] + (main[128:256] + more)
            for f in range(6):
                at = ((half * 2 + s) * 6 + f) * 128
                oq[at : at + 128, :] = done[:, f * 128 : f * 128 + 128]

        for half in range(2):
            turn = turns[every(half, 6, 2), :]
            swap, flip_a, flip_b = (turn & 4) != 0, (turn & 1) != 0, (turn & 2) != 0
            target = s * 6 * 242 + half
            source = (half * 2 + s) * 6 * 128
            for group in ORBITS:
                x = {n: oq[every(source + n[0] * 11 + n[1], 6, 128), :] for n in group}
                x = {(a, b): jnp.where(flip_a, x[last - a, b], x[a, b]) for a, b in group}
                x = {(a, b): jnp.where(flip_b, x[a, last - b], x[a, b]) for a, b in group}
                x = {(a, b): jnp.where(swap, x[b, a], x[a, b]) for a, b in group}
                for a, b in group:
                    face_out[every(target + 2 * (a * 11 + b), 6, 242), :] = x[a, b]
            mirror = turns[every(16 + half, 12, 2), :] != 0
            target = s * 12 * 22 + half
            source = (half * 2 + s) * EDGE_ROWS
            x = [ev[every(source + p, 12, 16), :] for p in range(NODES)]
            for p in range(NODES):
                edge_out[every(target + 2 * p, 12, 22), :] = jnp.where(mirror, x[last - p], x[p])
        rows = (slice(0, 1448), slice(1448, 2904))[s]
        copies.append(pltpu.make_async_copy(face_out.at[rows], face_hbm.at[rows], sems.at[2 * s]))
        rows = slice(s * 264, s * 264 + 264)
        copies.append(pltpu.make_async_copy(edge_out.at[rows], edge_hbm.at[rows], sems.at[2 * s + 1]))
        for copy in copies[2 * s : 2 * s + 2]:
            copy.start()
    for copy in copies:
        copy.wait()


VMEM = pl.BlockSpec(memory_space=pltpu.VMEM)
HBM = pl.BlockSpec(memory_space=pltpu.HBM)


def call(kernel, name, args, ins, outs, out_specs, scratch=(), sems=(), flops=0,
         limit=VMEM_LIMIT):
    shapes = [jax.ShapeDtypeStruct(o, F32) if isinstance(o, tuple) else o for o in outs]
    held = [pltpu.VMEM(o, F32) if isinstance(o, tuple) else o for o in scratch]
    held += [pltpu.SemaphoreType.DMA(n) for n in sems]
    size = sum(int(np.prod(a.shape)) * 4 for a in args)
    return pl.pallas_call(
        kernel,
        out_shape=shapes,
        in_specs=ins,
        out_specs=out_specs,
        scratch_shapes=held,
        compiler_params=pltpu.CompilerParams(vmem_limit_bytes=limit),
        cost_estimate=pl.CostEstimate(flops=flops, bytes_accessed=size, transcendentals=0),
        name=name,
    )(*args)


def per_device(face_residual, edge_residual, vertex_residual, face_orient, edge_orient, stiffness,
               face_basis, face_eigs, extension, edge_diag, element_heights):
    face = face_residual.reshape(2904, 128)
    edge = edge_residual.reshape(528, 128)
    vert = vertex_residual.reshape(32, 128)
    fturn = face_orient.reshape(6, 2, 128)
    eturn = edge_orient.reshape(24, 128)
    stiff = stiffness.reshape(2, 128)
    tiles = 24 * 128
    kept = [(tiles, 128), (4 * EDGE_ROWS, 128), (4 * SIDE_ROWS, 128), (4 * SIDE_ROWS, 128),
            (128, 128), (128, 128), (128 * SENT, 128), (40, 128), (2, 128)]
    kinds = [F32] * 7 + [jnp.int32, F32]
    xf, ef, near, far, zp, zm, cb, turns, weights = call(
        first_kernel, "frame", (face, edge, vert, fturn, eturn, stiff), [HBM] * 6,
        [jax.ShapeDtypeStruct(o, kind) for o, kind in zip(kept, kinds)], [HBM] * 9,
        [pltpu.VMEM(o, kind) for o, kind in zip(kept, kinds)]
        + [(2904, 128), (528, 128), (32, 128), pltpu.VMEM((6, 2, 128), jnp.int32)],
        ((7,), (21,)), limit=VMEM_WHOLE)
    up = lambda n: [(i, (i + 1) % n) for i in range(n)]
    down = lambda n: [((i + 1) % n, i) for i in range(n)]
    swapped = lambda first: [p for i in range(first, first + SPLIT_X, 2)
                             for p in ((i, (i + 1) % SPLIT_X), ((i + 1) % SPLIT_X, i))]
    near = lax.ppermute(near, "gx", swapped(0))
    far = lax.ppermute(far, "gx", swapped(1))
    table, lift, rdiag = call(
        parameter_kernel, "parameters",
        (jnp.asarray(TABLE), element_heights.reshape(1, LAYERS), edge_diag.reshape(1, NODES),
         face_basis, face_eigs.reshape(1, NODES), extension.T), [HBM] * 6,
        [(TABLE_ROWS, 128), jax.ShapeDtypeStruct((256, 256), BF16), (16, 128)], [VMEM] * 3,
        ((1, LAYERS), (1, NODES), (NODES, NODES), (1, NODES), (48, FACE_NODES), (256, 128)), ((6,),))
    g = lax.all_to_all(cb.reshape(128, 3, 4, 128), ("gx", "gz"), 0, 0)
    g = g.reshape(128 * SENT, 128)
    zp, zm = call(corner_kernel, "corners", (zp, zm, near, far), [VMEM] * 4,
                  [(128, 128), (128, 128)], [VMEM] * 2, flops=CORNER_FLOPS)
    rzm = lax.ppermute(zp, "gz", up(SPLIT_Z))
    rzp = lax.ppermute(zm, "gz", down(SPLIT_Z))
    v, v_out, vb = call(
        solve_kernel, "coarse", (g, table), [VMEM] * 2, [(32, 128), (32, 128), (192, 128)],
        [VMEM, HBM, VMEM],
        ((2048, 128), (512, 128), (LEVELS * 16, 128), (1024, 128), (256, 128)), ((),),
        flops=200_000_000)
    face_out, edge_out = call(
        final_kernel, "finish",
        (xf, ef, near, far, rzm, rzp, weights, v, vb, lift, rdiag, turns), [VMEM] * 12,
        [(2904, 128), (528, 128)], [HBM] * 2,
        ((tiles, 128), (4 * EDGE_ROWS, 128), (2904, 128), (528, 128)), ((4,),))
    return (face_out.reshape(face_residual.shape), edge_out.reshape(edge_residual.shape),
            v_out.reshape(vertex_residual.shape))


def solution(mesh):
    columns = P(None, None, None, "gx", "gz")
    placed = (columns, columns, P(None, None, "gx", "gz"), P(None, "gx", "gz"),
              P(None, "gx", "gz"), P("gx", "gz"), P(), P(), P(), P(), P())
    return jax.shard_map(
        per_device, mesh=mesh, in_specs=placed,
        out_specs=(columns, columns, P(None, None, "gx", "gz")), check_vma=False)
```

```python
import math

import jax
import jax.numpy as jnp
import numpy as np
from jax import lax
from jax.experimental import pallas as pl
from jax.experimental.pallas import tpu as pltpu
from jax.sharding import PartitionSpec as P

F32 = jnp.float32
BF16 = jnp.bfloat16
HIGHEST = lax.Precision.HIGHEST
SHIFT_MASS = 0.004
NX, NZ, LAYERS, LEVELS, NODES = 16, 64, 32, 33, 11
SPLIT_X, SPLIT_Z, OWN_Z = 16, 8, 8
FACE_NODES = 121
EDGE_ROWS = 16 * 12
SIDE_ROWS = 192
SENT = 12
STATION = SENT * SPLIT_Z
VMEM_LIMIT = 24 * 1024 * 1024
CORNER_FLOPS = 100_000_000_000
VMEM_WHOLE = 60 * 1024 * 1024

FACE_SLOTS = ((-1, 0, 0), (1, 0, 0), (0, -1, 0), (0, 1, 0), (0, 0, -1), (0, 0, 1))
EDGE_SLOTS = (
    (0, -1, -1), (0, -1, 1), (0, 1, -1), (0, 1, 1),
    (-1, 0, -1), (-1, 0, 1), (1, 0, -1), (1, 0, 1),
    (-1, -1, 0), (-1, 1, 0), (1, -1, 0), (1, 1, 0),
)
VERTEX_SLOTS = tuple((x, z, y) for x in (-1, 1) for z in (-1, 1) for y in (-1, 1))
SENT_XP, SENT_XM = (6, 7, 10, 11), (4, 5, 8, 9)
SENT_ZP, SENT_ZM = (2, 3, 9, 11), (0, 1, 8, 10)


def orbits():
    seen, result = set(), []
    last = NODES - 1
    for a in range(NODES):
        for b in range(NODES):
            if (a, b) in seen:
                continue
            group, queue = [], [(a, b)]
            while queue:
                node = queue.pop()
                if node in seen:
                    continue
                seen.add(node)
                group.append(node)
                p, q = node
                queue += [(q, p), (last - p, q), (p, last - q)]
            result.append(group)
    return result


ORBITS = orbits()


def face_frame(slot):
    tangents = [axis for axis in range(3) if slot[axis] == 0]
    edges, corners = [], []
    for axis in tangents:
        for sign in (-1, 1):
            corner = list(slot)
            corner[axis] = sign
            edges.append(EDGE_SLOTS.index(tuple(corner)))
    for first in (-1, 1):
        for second in (-1, 1):
            corner = list(slot)
            corner[tangents[0]] = first
            corner[tangents[1]] = second
            corners.append(VERTEX_SLOTS.index(tuple(corner)))
    return edges, corners


def edge_ends(slot):
    axis = slot.index(0)
    ends = []
    for sign in (-1, 1):
        point = list(slot)
        point[axis] = sign
        ends.append(VERTEX_SLOTS.index(tuple(point)))
    return ends


def hartley_table(size):
    phase = np.outer(np.arange(size), np.arange(size)) % size
    angle = 2.0 * np.pi / size * phase
    return (np.cos(angle) + np.sin(angle)) / math.sqrt(size)


HX, HZ = hartley_table(NX), hartley_table(NZ)


def build_tables():
    f32 = lambda a: np.ascontiguousarray(a, dtype=np.float32)
    tables = {}
    forward = np.zeros((128, 2 * NZ))
    top_z = np.zeros((3, 128, 2 * NZ))
    for gz in range(SPLIT_Z):
        for kk in range(9):
            column = HZ[:, (8 * gz + kk) % NZ]
            forward[gz * SENT + kk] = np.tile(column, 2)
            top_z[kk // 3, gz * SENT + 9 + kk % 3] = np.tile(column, 2)
    tables["forward"] = f32(forward)
    tables["top_z"] = f32(top_z.reshape(3 * 128, 128))
    lane = np.arange(128)
    lane_s, lane_bx, lane_j = lane // 64, lane // 32 % 2, lane % 32
    mix = np.zeros((NX // 2, NX, 2, NZ))
    for k in range(NX):
        for x in range(NX):
            mix[k // 2, x, k % 2] = HX[k, x]
    tables["mix"] = f32(mix.reshape(NX * NX // 2, 128))
    top_x = np.zeros((2, 2, 16, 128))
    modes = np.zeros((16, 128))
    waves_x = 2.0 - 2.0 * np.cos(2.0 * np.pi / NX * np.arange(NX))
    waves_z = 2.0 - 2.0 * np.cos(2.0 * np.pi / NZ * np.arange(NZ))
    for row in range(16):
        s = row // 8
        for pair in range(2):
            k = row % 8 * 2 + pair
            for odd in range(2):
                x = 2 * (lane_j % 8) + odd
                top_x[odd, pair, row] = np.where(lane_s == s, HX[k, (x + lane_bx) % NX], 0.0)
            modes[row, pair * 64 : pair * 64 + 64] = waves_x[k] + waves_z + SHIFT_MASS
    tables["top_x"] = f32(top_x.reshape(64, 128))
    tables["modes"] = f32(modes)
    back_z = np.zeros((SPLIT_Z, 16, 2 * NZ))
    for gz in range(SPLIT_Z):
        for kk in range(9):
            back_z[gz, kk] = np.tile(HZ[(8 * gz + kk) % NZ], 2)
    tables["back_z"] = f32(back_z.reshape(SPLIT_Z * 16, 128))
    back_x = np.zeros((SPLIT_X, 2, 8, 2, NZ))
    for gx in range(SPLIT_X):
        for bx in range(2):
            for k in range(NX):
                back_x[gx, bx, k // 2, k % 2] = HX[(gx + bx) % NX, k]
    tables["back_x"] = f32(back_x.reshape(SPLIT_X * 16, 128))
    pick = np.zeros((32 + 192, 256))

    def fill(row, s, corner, half):
        bx, bz, by = corner // 4, corner // 2 % 2, corner % 2
        base = (((s * 2 + bx) * 2 + by) * 2 + bz) * 16
        for k in range(4):
            pick[row, base + half * 4 + k + bz] = 1.0

    for s in range(2):
        for half in range(2):
            for corner in range(8):
                fill((s * 8 + corner) * 2 + half, s, corner, half)
            for face, slot in enumerate(FACE_SLOTS):
                for place, corner in enumerate(face_frame(slot)[1]):
                    fill(32 + ((half * 2 + s) * 6 + face) * 8 + place, s, corner, half)
    tables["pick"] = f32(pick)
    expand = np.zeros((2, 128, NODES))
    for q in range(FACE_NODES):
        expand[0, q, q // NODES] = 1.0
        expand[1, q, q % NODES] = 1.0
    tables["cols_a"], tables["cols_b"] = f32(expand[0].T), f32(expand[1].T)
    for name in ("pick",):
        wide = tables.pop(name)
        tables[name + "_0"], tables[name + "_1"] = f32(wide[:, :128]), f32(wide[:, 128:])
    rows, places, pieces = 0, {}, []
    for name, value in tables.items():
        count = -(-value.shape[0] // 16) * 16
        places[name] = slice(rows, rows + value.shape[0])
        pieces.append(np.pad(value, ((0, count - value.shape[0]), (0, 0))))
        rows += count
    return f32(np.concatenate(pieces, axis=0)), places


TABLE, PLACE = build_tables()
PIVOTS = TABLE.shape[0]
CARRY = PIVOTS + LEVELS * 16
BACK = CARRY + LEVELS * 16
TABLE_ROWS = BACK + LAYERS * 16


def lanes_of(shape):
    return lax.broadcasted_iota(jnp.int32, shape, 1)


def rows_of(shape):
    return lax.broadcasted_iota(jnp.int32, shape, 0)


def roll(value, shift):
    return pltpu.roll(value, shift % 128, 1)


def every(start, size, stride):
    return pl.ds(start, size, stride=stride)


def from_below(low, high=None):
    lane = lanes_of(low.shape)
    return jnp.where(lane % 32 > 0, roll(low, 1), 0.0)


def from_above(value):
    lane = lanes_of(value.shape)
    return jnp.where(lane % 32 < 31, roll(value, -1), 0.0)


def from_before(pair, halo):
    first, second = roll(pair[0], 32), roll(pair[1], 32)
    head = lanes_of(first.shape) < 32
    return jnp.where(head, halo, first), jnp.where(head, first, second)


def from_after(pair, halo):
    first, second = roll(pair[0], 96), roll(pair[1], 96)
    tail = lanes_of(first.shape) >= 96
    return jnp.where(tail, second, first), jnp.where(tail, halo, second)


def coarse_block(vert, station):
    small = (8, 128)
    lane8, row8 = lanes_of(small), rows_of(small)
    group8 = lane8 // 32
    big = (16, 128)
    lane, row = lanes_of(big), rows_of(big)
    group = lane // 32
    low = [vert[every(half, 8, 4), :] for half in range(2)]
    high = [vert[every(2 + half, 8, 4), :] for half in range(2)]

    def turned(halves):
        parts = []
        for half in range(2):
            for turn in range(4):
                moved = roll(halves[half], 32 * turn)
                for bz in range(2):
                    mask = (group8 == row8 // 2) & (row8 % 2 == bz)
                    total = jnp.sum(jnp.where(mask, moved, 0.0), axis=0, keepdims=True)
                    parts.append((half, turn, bz, jnp.broadcast_to(total, big)))
        return parts

    def spread(parts, point, valid):
        out = jnp.zeros(big, F32)
        for half, turn, bz, total in parts:
            k = point - bz
            mask = (k >= 4 * half) & (k < 4 * half + 4) & (((group - k + 8) % 4) == turn) & valid
            out = out + jnp.where(mask, total, 0.0)
        return out

    main = turned([low[half] + from_below(high[half]) for half in range(2)])
    top = turned(high)
    block = spread(main, row, row < 9)
    last = lane % 32 == 31
    for third in range(3):
        moved = spread(top, row - 9 + 3 * third, (row >= 9) & (row < SENT))
        moved = jnp.where(last, moved, 0.0)
        block = block + pltpu.roll(moved, station // 2 + 8 * third + 97, 1)
    return block


def first_kernel(face_in, edge_in, vert_in, fturn_in, eturn_in, stiff_in,
                 xf_out, ef_out, near_out, far_out, zp_out, zm_out, cb_out, turns_out, weights_out,
                 xf, ef, near, far, zp, zm, cb, turns, weights,
                 face, edge, vert, fturn, sems, out_sems):
    copies = [
        pltpu.make_async_copy(source, target, sems.at[at])
        for at, (source, target) in enumerate((
            (vert_in, vert),
            (fturn_in, fturn),
            (eturn_in, turns.at[16:40]),
            (stiff_in, weights),
            (face_in.at[0:1456], face.at[0:1456]),
            (edge_in, edge),
            (face_in.at[1456:2904], face.at[1456:2904]),
        ))
    ]
    sent = []

    def send(source, target):
        copy = pltpu.make_async_copy(source, target, out_sems.at[len(sent)])
        copy.start()
        sent.append(copy)

    for copy in copies:
        copy.start()
    copies[0].wait()
    block = coarse_block(vert, lax.axis_index("gx"))
    for device in range(128):
        cb[device * SENT : device * SENT + SENT, :] = block[0:SENT]
    send(cb, cb_out)
    for at in (1, 2, 3, 5):
        copies[at].wait()
    for f in range(6):
        turns[2 * f : 2 * f + 2, :] = fturn[f]
    turns[12:16, :] = jnp.zeros((4, 128), jnp.int32)
    send(turns, turns_out)
    send(weights, weights_out)
    stiff = weights

    last = NODES - 1
    first_core = lax.axis_index("gx") % 2 == 0
    mirrors, masks = [], []
    for half in range(2):
        turn = turns[every(half, 6, 2), :]
        masks.append(((turn & 4) != 0, (turn & 1) != 0, (turn & 2) != 0))
        mirrors.append(turns[every(16 + half, 12, 2), :] != 0)
    for half in range(2):
        for s in range(2):
            if half == 0:
                copies[4 + 2 * s].wait()
            swap, flip_a, flip_b = masks[half]
            source = s * 6 * 242 + half
            tile = half * 2 + s
            target = tile * 6 * 128
            for group in ORBITS:
                x = {n: face[every(source + 2 * (n[0] * 11 + n[1]), 6, 242), :] for n in group}
                x = {(a, b): jnp.where(swap, x[b, a], x[a, b]) for a, b in group}
                x = {(a, b): jnp.where(flip_a, x[last - a, b], x[a, b]) for a, b in group}
                x = {(a, b): jnp.where(flip_b, x[a, last - b], x[a, b]) for a, b in group}
                for a, b in group:
                    xf[every(target + a * 11 + b, 6, 128), :] = x[a, b]
            for pad in range(121, 128):
                xf[every(target + pad, 6, 128), :] = jnp.zeros((6, 128), F32)
            send(xf.at[target : target + 768], xf_out.at[target : target + 768])
            source = s * 12 * 22 + half
            target = tile * EDGE_ROWS
            x = [edge[every(source + 2 * p, 12, 22), :] for p in range(NODES)]
            for p in range(NODES):
                ef[every(target + p, 12, 16), :] = jnp.where(mirrors[half], x[last - p], x[p])
            for pad in range(NODES, 16):
                ef[every(target + pad, 12, 16), :] = jnp.zeros((12, 128), F32)
            send(ef.at[target : target + EDGE_ROWS], ef_out.at[target : target + EDGE_ROWS])
            base = tile * SIDE_ROWS
            up = xf[(tile * 6 + 1) * 128 : (tile * 6 + 2) * 128, :]
            down = xf[tile * 6 * 128 : (tile * 6 + 1) * 128, :]
            near[base : base + 128, :] = jnp.where(first_core, up, down)
            far[base : base + 128, :] = jnp.where(first_core, down, up)
            for ref in (near, far):
                ref[base + 127 : base + 128, :] = stiff[half : half + 1, :]
            for place in range(4):
                up_at = (tile * 12 + SENT_XP[place]) * 16
                down_at = (tile * 12 + SENT_XM[place]) * 16
                up, down = ef[up_at : up_at + 16, :], ef[down_at : down_at + 16, :]
                at = base + 128 + place * 16
                near[at : at + 16, :] = jnp.where(first_core, up, down)
                far[at : at + 16, :] = jnp.where(first_core, down, up)
            for ref, out in ((near, near_out), (far, far_out)):
                send(ref.at[base : base + SIDE_ROWS], out.at[base : base + SIDE_ROWS])

    for ref, half, slot, edges in ((zp, 1, 3, SENT_ZP), (zm, 0, 2, SENT_ZM)):
        own = 96 if half else 0
        group = lanes_of((128, 128)) // 32
        faces = [
            roll(xf[((half * 2 + s) * 6 + slot) * 128 : ((half * 2 + s) * 6 + slot + 1) * 128, :],
                 32 * s - own)
            for s in range(2)
        ]
        lines = jnp.concatenate(
            [ef[((half * 2 + s) * 12 + e) * 16 : ((half * 2 + s) * 12 + e + 1) * 16, :]
             for s in range(2) for e in edges],
            axis=0,
        )
        weight = jnp.broadcast_to(roll(stiff[half : half + 1, :], 96 - own), (128, 128))
        out = jnp.where(group == 0, faces[0], faces[1])
        out = jnp.where(group == 2, roll(lines, 64 - own), out)
        ref[...] = jnp.where(group == 3, weight, out)
    send(zp, zp_out)
    send(zm, zm_out)
    for copy in sent:
        copy.wait()


class Side:
    def __init__(self, first, second):
        self.first, self.second = first, second
        self.core = lax.axis_index("gx") % 2 == 0

    def __getitem__(self, at):
        return jnp.where(self.core, self.first[at], self.second[at])


def corner_kernel(zp, zm, near, far, out_p, out_m):
    rxm, rxp = Side(far, near), Side(near, far)
    lane, row = lanes_of((128, 128)), rows_of((128, 128))
    group = lane // 32
    for ref, out, half, place in ((zp, out_p, 1, 3), (zm, out_m, 0, 2)):
        own = 96 if half else 0
        out[...] = ref[...]
        for s in range(2):
            base = (half * 2 + s) * SIDE_ROWS + 128 + place * 16
            for third, side in ((2, rxm), (3, rxp)):
                at = s * 64 + third * 16
                moved = roll(side[base : base + 16, :], 64 - own)
                keep = lanes_of((16, 128)) // 32 == 2
                out[at : at + 16, :] += jnp.where(keep, moved, 0.0)
        for r, side in ((1, rxm), (2, rxp)):
            base = half * 2 * SIDE_ROWS + 127
            moved = roll(side[base : base + 1, :], 96 - own)
            out[r : r + 1, :] += jnp.where(lanes_of((1, 128)) >= 96, moved, 0.0)


def parameter_kernel(table_in, heights_in, diag_in, basis_in, eigs_in, ext_in,
                     table, lift, rdiag, heights, diag, basis, eigs, ext, work, sems):
    copies = [
        pltpu.make_async_copy(source, target, sems.at[at])
        for at, (source, target) in enumerate((
            (heights_in, heights), (diag_in, diag), (basis_in, basis), (eigs_in, eigs),
            (ext_in, ext), (table_in, table.at[0:PIVOTS]),
        ))
    ]
    for copy in copies:
        copy.start()
    for copy in copies:
        copy.wait()

    def dot(x, y):
        return jnp.dot(x, y, precision=HIGHEST, preferred_element_type=F32)

    def dot_first(x, y):
        return lax.dot_general(x, y, (((0,), (0,)), ((), ())), precision=HIGHEST,
                               preferred_element_type=F32)

    b = basis[...]
    cols_a, cols_b = table[PLACE["cols_a"], :], table[PLACE["cols_b"], :]
    modes = table[PLACE["modes"], :]
    kron = dot(dot_first(cols_a, b), cols_a) * dot(dot_first(cols_b, b), cols_b)
    scale = dot(eigs[...], cols_a + cols_b)
    scale = 1.0 / jnp.where(lanes_of((1, 128)) < FACE_NODES, scale, 1.0)
    work[...] = jnp.zeros((256, 128), F32)
    work[0:128, :] = lax.dot_general(
        kron * scale, kron, (((1,), (1,)), ((), ())), precision=HIGHEST,
        preferred_element_type=F32,
    )
    for place in range(4):
        work[128 + 16 * place : 139 + 16 * place, 0:FACE_NODES] = ext[11 * place : 11 * place + 11, :]
    work[192:196, 0:FACE_NODES] = ext[44:48, :]
    full = work[...].T
    high = full.astype(BF16)
    lift[0:128, :] = high
    lift[128:256, :] = (full - high.astype(F32)).astype(BF16)
    row = rows_of((16, 128))
    nodes = jnp.ones((16, 128), F32)
    for p in range(NODES):
        nodes = jnp.where(row == p, diag[0:1, p : p + 1], nodes)
    rdiag[...] = 1.0 / nodes

    tall = [jnp.broadcast_to(heights[0:1, l : l + 1], (16, 128)) for l in range(LAYERS)]
    inverse = [1.0 / h for h in tall]
    prime = None
    for l in range(LEVELS):
        if l == 0:
            stiff, mass = inverse[0], 0.5 * tall[0]
        elif l == LAYERS:
            stiff, mass = inverse[l - 1], 0.5 * tall[l - 1]
        else:
            stiff, mass = inverse[l - 1] + inverse[l], 0.5 * (tall[l - 1] + tall[l])
        pivot = stiff + modes * mass
        if l:
            pivot = pivot - inverse[l - 1] * prime
        rp = 1.0 / pivot
        table[PIVOTS + l * 16 : PIVOTS + l * 16 + 16, :] = rp
        if l:
            table[CARRY + l * 16 : CARRY + l * 16 + 16, :] = inverse[l - 1] * rp
        else:
            table[CARRY : CARRY + 16, :] = jnp.zeros((16, 128), F32)
        if l < LAYERS:
            prime = inverse[l] * rp
            table[BACK + l * 16 : BACK + l * 16 + 16, :] = prime


def thirds(value):
    high = value.astype(BF16)
    rest = value - high.astype(F32)
    middle = rest.astype(BF16)
    return high, middle, (rest - middle.astype(F32)).astype(BF16)


def solve_kernel(g, table, v_out, vb_out, tz, zs, vs, ss, cs):
    def dot(x, y):
        return jnp.dot(x, y, precision=HIGHEST, preferred_element_type=F32)

    pad = jnp.zeros((128 - STATION, 128), F32)
    stations = []
    for x in range(NX):
        station = g[x * STATION : x * STATION + STATION, :]
        stations.append(jnp.concatenate([station, pad], axis=0).T)
    high, middle, low = thirds(jnp.concatenate(stations, axis=0))
    wave = thirds(table[PLACE["forward"], :])
    both = jnp.concatenate(wave[0:2], axis=1)
    main = jnp.dot(jnp.concatenate([high, middle], axis=1), jnp.concatenate([both, both], axis=0),
                   preferred_element_type=F32)
    more = jnp.dot(jnp.concatenate([high, low], axis=1),
                   jnp.concatenate([wave[2], wave[0]], axis=0), preferred_element_type=F32)
    tz[...] = main[:, 0:128] + (main[:, 128:256] + more)
    third = rows_of((128, 128)) % 32 // 8
    base_z, base_x = PLACE["top_z"].start, PLACE["top_x"].start
    tops = None
    for odd in range(2):
        total = stations[odd]
        for x in range(odd + 2, NX, 2):
            total = total + stations[x]
        parts = [dot(total, table[base_z + 128 * q : base_z + 128 * q + 128, :]) for q in range(3)]
        part = jnp.where(third == 0, parts[0], jnp.where(third == 1, parts[1], parts[2]))
        part = dot(table[base_x + 32 * odd : base_x + 32 * odd + 32, :], part)
        tops = part if tops is None else tops + part
    mix = PLACE["mix"].start
    top = jnp.where(lanes_of((16, 128)) < 64, tops[0:16], tops[16:32])

    for s in range(2):
        for j in (0, 16):
            at = s * 64 + j
            parts = []
            for x in range(NX):
                near, far = x * 128 + at, (x + NX - 1) % NX * 128 + at + 32
                parts.append(tz[near : near + 16, :] + tz[far : far + 16, :])
            for pair in range(NX // 2):
                row = mix + pair * NX
                acc = parts[0] * table[row : row + 1, :]
                for x in range(1, NX):
                    acc = acc + parts[x] * table[row + x : row + x + 1, :]
                to = (s * 8 + pair) * 32 + j
                zs[to : to + 16, :] = acc

    value = None
    for l in range(LEVELS):
        rhs = zs[every(l, 16, 32), :] if l < LAYERS else top
        at = l * 16
        step = rhs * table[PIVOTS + at : PIVOTS + at + 16, :]
        value = step if l == 0 else step + table[CARRY + at : CARRY + at + 16, :] * value
        vs[at : at + 16, :] = value
    for l in range(LEVELS - 1, -1, -1):
        if l < LEVELS - 1:
            at = l * 16
            value = vs[at : at + 16, :] + table[BACK + at : BACK + at + 16, :] * value
        ss[every(l, 16, 64), :] = value
    for l in range(LEVELS, 40):
        ss[every(l, 16, 64), :] = jnp.zeros((16, 128), F32)

    at = PLACE["back_x"].start + lax.axis_index("gx") * 16
    hx = table[pl.ds(pl.multiple_of(at, 16), 16), :]
    columns = []
    for s in range(2):
        for bx in range(2):
            acc = None
            for t in range(8):
                r = bx * 8 + t
                term = ss[(s * 8 + t) * 64 : (s * 8 + t) * 64 + 40, :] * hx[r : r + 1, :]
                acc = term if acc is None else acc + term
            columns += [acc, jnp.zeros((24, 128), F32)]
    at = PLACE["back_z"].start + lax.axis_index("gz") * 16
    hz = table[pl.ds(pl.multiple_of(at, 16), 16), :]
    q = lax.dot_general(hz, jnp.concatenate(columns, axis=0), (((1,), (1,)), ((), ())),
                        precision=HIGHEST, preferred_element_type=F32)
    lane, row = lanes_of((16, 128)), rows_of((16, 128))
    group = lane // 32
    for s in range(2):
        near = q[:, s * 128 : s * 128 + 128]
        far = roll(near, 64)
        for bx in range(2):
            acc = jnp.where((lane < 64) == (bx == 0), near, far)
            for by in range(2):
                plain = roll(acc, 127) if by else acc
                moved = roll(plain, 32)
                mixed = jnp.where(group % 2 == 1, moved, plain)
                for bz in range(2):
                    base = (((s * 2 + bx) * 2 + by) * 2 + bz) * 16
                    keep = (row - bz + 4) % 4 == group
                    cs[base : base + 16, :] = jnp.where(keep, mixed, 0.0)
    pick = jnp.concatenate(
        [table[PLACE["pick_0"], :].astype(BF16), table[PLACE["pick_1"], :].astype(BF16)], axis=1)
    rest, picked = cs[...], None
    for _ in range(3):
        part = rest.astype(BF16)
        rest = rest - part.astype(F32)
        chosen = jnp.dot(pick, part, preferred_element_type=F32)
        picked = chosen if picked is None else picked + chosen
    v_out[...] = picked[0:32]
    vb_out[...] = picked[32:224]


def final_kernel(xf, ef, near, far, rzm, rzp, stiff, v, vb, lift, rdiag, turns,
                 face_hbm, edge_hbm, v_hbm, oq, ev, face_out, edge_out, sems):
    last = NODES - 1
    vertex_copy = pltpu.make_async_copy(v, v_hbm, sems.at[4])
    vertex_copy.start()
    rxm, rxp = Side(far, near), Side(near, far)
    w = [stiff[half : half + 1, :] for half in range(2)]

    def tile(half, s, f):
        at = ((half * 2 + s) * 6 + f) * 128
        return xf[at : at + 128, :]

    def line(half, s, e):
        at = ((half * 2 + s) * 12 + e) * 16
        return ef[at : at + 16, :]

    def side_face(ref, half, s):
        at = (half * 2 + s) * SIDE_ROWS
        return ref[at : at + 128, :]

    def side_line(ref, half, s, place):
        at = (half * 2 + s) * SIDE_ROWS + 128 + place * 16
        return ref[at : at + 16, :]

    def side_weight(ref, half):
        at = half * 2 * SIDE_ROWS + 127
        return ref[at : at + 1, :]

    def halo_line(ref, s, place, to):
        at = s * 64 + place * 16
        return roll(ref[at : at + 16, :], to - 64)

    wxm = [w[half] + side_weight(rxm, half) for half in range(2)]
    wxp = [w[half] + side_weight(rxp, half) for half in range(2)]
    wzm_in = [roll(rzm[r : r + 1, :], 32) for r in range(3)]
    wzp_in = [rzp[r : r + 1, :] for r in range(3)]

    def add_before(pair, halo):
        moved = from_before(pair, halo)
        return [pair[0] + moved[0], pair[1] + moved[1]]

    def add_after(pair, halo):
        moved = from_after(pair, halo)
        return [pair[0] + moved[0], pair[1] + moved[1]]

    wzm, wzp = add_before(w, wzm_in[0]), add_after(w, wzp_in[0])
    corner = [add_before(wxm, wzm_in[1]), add_after(wxm, wzp_in[1]),
              add_before(wxp, wzm_in[2]), add_after(wxp, wzp_in[2])]
    below = lambda pair: [x + from_below(x) for x in pair]
    above = lambda pair: [x + from_above(x) for x in pair]
    covers = [below(wzm), above(wzm), below(wzp), above(wzp),
              below(wxm), above(wxm), below(wxp), above(wxp)] + corner
    face_covers = [wxm, wxp, wzm, wzp, below(w), above(w)]
    rec_face = [[1.0 / x for x in pair] for pair in face_covers]
    rec_edge = [[1.0 / x for x in pair] for pair in covers]

    row16 = rows_of((16, 128))
    high_t = (row16 + 1).astype(F32) / (NODES + 1.0)
    low_t = 1.0 - high_t
    diag = rdiag[...]
    copies = []

    for s in range(2):
        e = {}
        for half in range(2):
            for k in range(4):
                e[k, half] = line(half, s, k)
            for k, place in ((4, 0), (5, 1), (8, 2), (9, 3)):
                e[k, half] = line(half, s, k) + side_line(rxm, half, s, place)
            for k, place in ((6, 0), (7, 1), (10, 2), (11, 3)):
                e[k, half] = line(half, s, k) + side_line(rxp, half, s, place)
        both = lambda k: (e[k, 0], e[k, 1])
        sums = {}
        for k, other, place in ((0, 2, 0), (1, 3, 1), (8, 9, 2), (10, 11, 3)):
            moved = from_before(both(other), halo_line(rzm, s, place, 0))
            for half in range(2):
                sums[k, half] = e[k, half] + moved[half]
        for k, other, place in ((2, 0, 0), (3, 1, 1), (9, 8, 2), (11, 10, 3)):
            moved = from_after(both(other), halo_line(rzp, s, place, 96))
            for half in range(2):
                sums[k, half] = e[k, half] + moved[half]
        for k in range(4, 8):
            for half in range(2):
                sums[k, half] = e[k, half]
        for half in range(2):
            for k in range(0, 8, 2):
                a, b = sums[k, half], sums[k + 1, half]
                sums[k, half], sums[k + 1, half] = a + from_below(b), b + from_above(a)
            tilebase = (half * 2 + s) * EDGE_ROWS
            vertex = v[every(s * 16 + half, 8, 2), :]
            for k in range(12):
                start, stop = edge_ends(EDGE_SLOTS[k])
                local = sums[k, half] * (diag * rec_edge[k][half])
                ev[tilebase + k * 16 : tilebase + k * 16 + 16, :] = (
                    local + low_t * vertex[start : start + 1] + high_t * vertex[stop : stop + 1]
                )
        for half in range(2):
            columns = []
            for f in range(6):
                own = tile(half, s, f)
                if f == 0:
                    total = own + side_face(rxm, half, s)
                elif f == 1:
                    total = own + side_face(rxp, half, s)
                elif f == 2:
                    halo = roll(rzm[...], -32 * s)
                    total = own + from_before((tile(0, s, 3), tile(1, s, 3)), halo)[half]
                elif f == 3:
                    halo = roll(rzp[...], 96 - 32 * s)
                    total = own + from_after((tile(0, s, 2), tile(1, s, 2)), halo)[half]
                elif f == 4:
                    total = own + from_below(tile(half, s, 5))
                else:
                    total = own + from_above(tile(half, s, 4))
                edges = face_frame(FACE_SLOTS[f])[0]
                tilebase = (half * 2 + s) * EDGE_ROWS
                at = ((half * 2 + s) * 6 + f) * 8
                columns.append(jnp.concatenate(
                    [total * rec_face[f][half]]
                    + [ev[tilebase + k * 16 : tilebase + k * 16 + 16, :] for k in edges]
                    + [vb[at : at + 8, :], jnp.zeros((56, 128), F32)], axis=0))
            full = jnp.concatenate(columns, axis=1)
            high = full.astype(BF16)
            rest = (full - high.astype(F32)).astype(BF16)
            main = jnp.dot(lift[...], high, preferred_element_type=F32)
            more = jnp.dot(lift[0:128, :], rest, preferred_element_type=F32)
            done = main[0:128] + (main[128:256] + more)
            for f in range(6):
                at = ((half * 2 + s) * 6 + f) * 128
                oq[at : at + 128, :] = done[:, f * 128 : f * 128 + 128]

        for half in range(2):
            turn = turns[every(half, 6, 2), :]
            swap, flip_a, flip_b = (turn & 4) != 0, (turn & 1) != 0, (turn & 2) != 0
            target = s * 6 * 242 + half
            source = (half * 2 + s) * 6 * 128
            for group in ORBITS:
                x = {n: oq[every(source + n[0] * 11 + n[1], 6, 128), :] for n in group}
                x = {(a, b): jnp.where(flip_a, x[last - a, b], x[a, b]) for a, b in group}
                x = {(a, b): jnp.where(flip_b, x[a, last - b], x[a, b]) for a, b in group}
                x = {(a, b): jnp.where(swap, x[b, a], x[a, b]) for a, b in group}
                for a, b in group:
                    face_out[every(target + 2 * (a * 11 + b), 6, 242), :] = x[a, b]
            mirror = turns[every(16 + half, 12, 2), :] != 0
            target = s * 12 * 22 + half
            source = (half * 2 + s) * EDGE_ROWS
            x = [ev[every(source + p, 12, 16), :] for p in range(NODES)]
            for p in range(NODES):
                edge_out[every(target + 2 * p, 12, 22), :] = jnp.where(mirror, x[last - p], x[p])
        rows = (slice(0, 1448), slice(1448, 2904))[s]
        copies.append(pltpu.make_async_copy(face_out.at[rows], face_hbm.at[rows], sems.at[2 * s]))
        rows = slice(s * 264, s * 264 + 264)
        copies.append(pltpu.make_async_copy(edge_out.at[rows], edge_hbm.at[rows], sems.at[2 * s + 1]))
        for copy in copies[2 * s : 2 * s + 2]:
            copy.start()
    for copy in copies:
        copy.wait()
    vertex_copy.wait()


VMEM = pl.BlockSpec(memory_space=pltpu.VMEM)
HBM = pl.BlockSpec(memory_space=pltpu.HBM)


def call(kernel, name, args, ins, outs, out_specs, scratch=(), sems=(), flops=0,
         limit=VMEM_LIMIT):
    shapes = [jax.ShapeDtypeStruct(o, F32) if isinstance(o, tuple) else o for o in outs]
    held = [pltpu.VMEM(o, F32) if isinstance(o, tuple) else o for o in scratch]
    held += [pltpu.SemaphoreType.DMA(n) for n in sems]
    size = sum(int(np.prod(a.shape)) * 4 for a in args)
    return pl.pallas_call(
        kernel,
        out_shape=shapes,
        in_specs=ins,
        out_specs=out_specs,
        scratch_shapes=held,
        compiler_params=pltpu.CompilerParams(vmem_limit_bytes=limit),
        cost_estimate=pl.CostEstimate(flops=flops, bytes_accessed=size, transcendentals=0),
        name=name,
    )(*args)


def per_device(face_residual, edge_residual, vertex_residual, face_orient, edge_orient, stiffness,
               face_basis, face_eigs, extension, edge_diag, element_heights):
    face = face_residual.reshape(2904, 128)
    edge = edge_residual.reshape(528, 128)
    vert = vertex_residual.reshape(32, 128)
    fturn = face_orient.reshape(6, 2, 128)
    eturn = edge_orient.reshape(24, 128)
    stiff = stiffness.reshape(2, 128)
    tiles = 24 * 128
    kept = [(tiles, 128), (4 * EDGE_ROWS, 128), (4 * SIDE_ROWS, 128), (4 * SIDE_ROWS, 128),
            (128, 128), (128, 128), (128 * SENT, 128), (40, 128), (2, 128)]
    kinds = [F32] * 7 + [jnp.int32, F32]
    xf, ef, near, far, zp, zm, cb, turns, weights = call(
        first_kernel, "frame", (face, edge, vert, fturn, eturn, stiff), [HBM] * 6,
        [jax.ShapeDtypeStruct(o, kind) for o, kind in zip(kept, kinds)], [HBM] * 9,
        [pltpu.VMEM(o, kind) for o, kind in zip(kept, kinds)]
        + [(2904, 128), (528, 128), (32, 128), pltpu.VMEM((6, 2, 128), jnp.int32)],
        ((7,), (21,)), limit=VMEM_WHOLE)
    up = lambda n: [(i, (i + 1) % n) for i in range(n)]
    down = lambda n: [((i + 1) % n, i) for i in range(n)]
    swapped = lambda first: [p for i in range(first, first + SPLIT_X, 2)
                             for p in ((i, (i + 1) % SPLIT_X), ((i + 1) % SPLIT_X, i))]
    near = lax.ppermute(near, "gx", swapped(0))
    far = lax.ppermute(far, "gx", swapped(1))
    table, lift, rdiag = call(
        parameter_kernel, "parameters",
        (jnp.asarray(TABLE), element_heights.reshape(1, LAYERS), edge_diag.reshape(1, NODES),
         face_basis, face_eigs.reshape(1, NODES), extension.T), [HBM] * 6,
        [(TABLE_ROWS, 128), jax.ShapeDtypeStruct((256, 256), BF16), (16, 128)], [VMEM] * 3,
        ((1, LAYERS), (1, NODES), (NODES, NODES), (1, NODES), (48, FACE_NODES), (256, 128)), ((6,),))
    g = lax.all_to_all(cb.reshape(128, 3, 4, 128), ("gx", "gz"), 0, 0)
    g = g.reshape(128 * SENT, 128)
    zp, zm = call(corner_kernel, "corners", (zp, zm, near, far), [VMEM] * 4,
                  [(128, 128), (128, 128)], [VMEM] * 2, flops=CORNER_FLOPS)
    rzm = lax.ppermute(zp, "gz", up(SPLIT_Z))
    rzp = lax.ppermute(zm, "gz", down(SPLIT_Z))
    v, vb = call(
        solve_kernel, "coarse", (g, table), [VMEM] * 2, [(32, 128), (192, 128)],
        [VMEM, VMEM],
        ((2048, 128), (512, 128), (LEVELS * 16, 128), (1024, 128), (256, 128)),
        flops=200_000_000)
    face_out, edge_out, v_out = call(
        final_kernel, "finish",
        (xf, ef, near, far, rzm, rzp, weights, v, vb, lift, rdiag, turns), [VMEM] * 12,
        [(2904, 128), (528, 128), (32, 128)], [HBM] * 3,
        ((tiles, 128), (4 * EDGE_ROWS, 128), (2904, 128), (528, 128)), ((5,),))
    return (face_out.reshape(face_residual.shape), edge_out.reshape(edge_residual.shape),
            v_out.reshape(vertex_residual.shape))


def solution(mesh):
    columns = P(None, None, None, "gx", "gz")
    placed = (columns, columns, P(None, None, "gx", "gz"), P(None, "gx", "gz"),
              P(None, "gx", "gz"), P("gx", "gz"), P(), P(), P(), P(), P())
    return jax.shard_map(
        per_device, mesh=mesh, in_specs=placed,
        out_specs=(columns, columns, P(None, None, "gx", "gz")), check_vma=False)
```
